32 devices in a mesh: grp: 4 (over y, x), dev: 8 (over z, core).
Axes of the slice: x: 2, y: 2, z: 4, core: 2. Of those that a mesh axis runs over, the one named last changes fastest.
Arguments:
- sketch: bfloat16 [65536, 256], P(('grp', 'dev')), may hold values from -4 to 4
- marginal_std: float32 [65536], P(('grp', 'dev')), may hold values from 0.1 to 10
- cov_tiles: bfloat16 [9, 256, 256], replicated, may hold values from 0 to 1
- tile_cols: int32 [256, 9], P(('grp', 'dev')), may hold values from -1 to 255, as said below
Outputs:
- basis: float32 [65536, 256], P(('grp', 'dev'))
- factor: float32 [256, 256], replicated
The draws below stay inside these ranges and needn't reach their ends.
Inputs may be any that keep to these rules, and one draw needn't show every extreme that they name: `tile_cols`: tile t holds one line of 256 cells. The lines lie in depth order, except that the order within each aligned block of 4 tiles is permuted. Entry e of the list of tile t is the tile that holds the line e - 4 lines from the line of t (entry 4 is t itself), or -1 where that line lies beyond the ends of the field.
All inputs are finite; a program needn't handle non-finite values.
Results may differ from the reference program's by a relative error of at most 0.0035.
Values may be sent and summed in bfloat16 or wider, within the bound.
No kernel may reach another device: no remote copies, remote signals or barrier semaphores. Data moves between devices by JAX's collectives and lax.ppermute only.
A program may use at most 64 MiB of HBM per device.

```python
import math
import jax
import jax.numpy as jnp
from jax import lax

TILE = 256
K = 256
RT = 8
REACH = 4
LAGS = 9
ROWS_DEV = 2048
TILES = 256
M = 65536


def draw_sketch(key, part):
    split_keys = jax.random.split(key, 2)
    column_scale = jnp.exp(jax.random.uniform(split_keys[0], (K,), jnp.float32, math.log(0.05), math.log(0.5)))
    values = jnp.clip(jax.random.normal(split_keys[1], (M, K), jnp.float32), -6.0, 6.0)
    return (values * column_scale[None, :]).astype(jnp.bfloat16)


def draw_marginal_std(key, part):
    first_key, second_key = jax.random.split(key)
    block_count = M // ROWS_DEV
    position = (jnp.arange(M, dtype=jnp.int32) // ROWS_DEV).astype(jnp.float32) / max(block_count - 1, 1)
    rise_factor = math.log(3.0)
    local_spread = math.log(2.0)
    block_noise = jax.random.uniform(first_key, (block_count,), jnp.float32, -0.3, 0.3)
    row_noise = jax.random.uniform(second_key, (M,), jnp.float32, -local_spread, local_spread)
    return jnp.exp(rise_factor * (position - 0.5) + jnp.repeat(block_noise, ROWS_DEV) + row_noise)


def draw_cov_tiles(key, part):
    split_keys = jax.random.split(key, 4)
    dip_angle = jax.random.uniform(split_keys[0], (), jnp.float32, -0.5, 0.5)
    radius_along = jax.random.uniform(split_keys[1], (), jnp.float32, 0.6, 1.0)
    radius_across = jax.random.uniform(split_keys[2], (), jnp.float32, 0.9, 1.0)
    nugget = jax.random.uniform(split_keys[3], (), jnp.float32, 0.1, 0.3)
    lag_ids = jnp.arange(LAGS, dtype=jnp.int32) - REACH
    across = lag_ids.astype(jnp.float32) / (REACH + 1)
    cell_ids = jnp.arange(TILE, dtype=jnp.int32)
    along = (cell_ids[None, :] - cell_ids[:, None]).astype(jnp.float32) / (TILE / 4.0)
    first_axis = along[None, :, :] * jnp.cos(dip_angle) + across[:, None, None] * jnp.sin(dip_angle)
    second_axis = -along[None, :, :] * jnp.sin(dip_angle) + across[:, None, None] * jnp.cos(dip_angle)
    distance = jnp.sqrt((first_axis / radius_along) ** 2 + (second_axis / radius_across) ** 2)
    spherical = jnp.where(distance < 1.0, 1.0 - 1.5 * distance + 0.5 * distance ** 3, 0.0)
    same_cell = (lag_ids[:, None, None] == 0) & (cell_ids[:, None] == cell_ids[None, :])[None, :, :]
    values = (1.0 - nugget) * spherical + nugget * same_cell.astype(jnp.float32)
    return values.astype(jnp.bfloat16)


def draw_tile_cols(key, part):
    block_count = TILES // REACH
    slot_ids = jnp.arange(REACH, dtype=jnp.int32)
    scores = jax.random.randint(key, (block_count, REACH), 0, 4096, dtype=jnp.int32) * REACH + slot_ids[None, :]
    slot_lines = jnp.argsort(scores, axis=1).astype(jnp.int32)
    inverse = jnp.argsort(slot_lines, axis=1).astype(jnp.int32)
    tile_ids = jnp.arange(TILES, dtype=jnp.int32)
    block_start = tile_ids // REACH * REACH
    line_of_tile = block_start + slot_lines.reshape(-1)
    tile_of_line = block_start + inverse.reshape(-1)
    lag_ids = jnp.arange(LAGS, dtype=jnp.int32) - REACH
    target = line_of_tile[:, None] + lag_ids[None, :]
    inside = (target >= 0) & (target < TILES)
    safe_target = jnp.clip(target, 0, TILES - 1).astype(jnp.int32)
    return jnp.where(inside, tile_of_line[safe_target], -1).astype(jnp.int32)


def setup_inputs(seed: int = 0) -> dict:
    key_of = jax.random.split(jax.random.key(seed), 5)
    sketch = draw_sketch(jax.random.fold_in(key_of[4], 71), 0)
    marginal_std = draw_marginal_std(jax.random.fold_in(key_of[4], 71), 0)
    cov_tiles = draw_cov_tiles(jax.random.fold_in(key_of[4], 71), 0)
    tile_cols = draw_tile_cols(jax.random.fold_in(key_of[4], 71), 0)
    return dict(sketch=sketch, marginal_std=marginal_std, cov_tiles=cov_tiles, tile_cols=tile_cols)


def reference(sketch, marginal_std, cov_tiles, tile_cols):
    scaled = (sketch.astype(jnp.float32) * marginal_std[:, None]).astype(jnp.bfloat16)
    scaled_tiles = scaled.reshape(TILES, TILE, K)
    present = tile_cols >= 0
    safe_cols = jnp.where(present, tile_cols, 0).astype(jnp.int32)
    correlation = cov_tiles.astype(jnp.float32)

    def block_product(block_pair):
        block_cols, block_present = block_pair
        gathered = scaled_tiles[block_cols.T].astype(jnp.float32)
        gathered = jnp.where(block_present.T[:, :, None, None], gathered, 0.0)
        return jnp.einsum('eij,etjk->tik', correlation, gathered)
    block_count = TILES // RT
    products = lax.map(block_product, (safe_cols.reshape(block_count, RT, LAGS), present.reshape(block_count, RT, LAGS)))
    latent_field = products.reshape(M, K) * marginal_std[:, None]
    gram_matrix = jnp.dot(latent_field.T, latent_field, precision=lax.Precision.HIGHEST) / M
    lower_factor = jnp.linalg.cholesky(gram_matrix)
    basis = lax.linalg.triangular_solve(lower_factor, latent_field, left_side=False, lower=True, transpose_a=True)
    return (basis, lower_factor.T)
```

```python
import functools

import jax
import jax.numpy as jnp
from jax import lax
from jax.experimental import pallas as pl
from jax.experimental.pallas import tpu as pltpu
from jax.sharding import PartitionSpec as P

AXES = ("grp", "dev")
F32 = jnp.float32
BF16 = jnp.bfloat16
LANES = 128
SUBLANES = 8
VMEM_LIMIT = 48 * 1024 * 1024


def rows_dot(left, right):
    return lax.dot_general(left, right, (((0,), (0,)), ((), ())), preferred_element_type=F32)


def split2(value):
    high = value.astype(BF16)
    return high, (value - high.astype(F32)).astype(BF16)


def split3(value):
    high = value.astype(BF16)
    rest = value - high.astype(F32)
    middle = rest.astype(BF16)
    return high, middle, (rest - middle.astype(F32)).astype(BF16)


def as_column(vector, width):
    count = vector.shape[1]
    parts = [
        jnp.broadcast_to(vector[:, i : i + LANES], (LANES, LANES)).T for i in range(0, count, LANES)
    ]
    column = jnp.concatenate(parts, axis=0)
    return jnp.concatenate([column] * (width // LANES), axis=1)


def own_tile(cols_ref, odd, line, reach):
    count = 2 * reach
    line = jnp.where(odd == 1, count - 1 - line, line)
    half = line // reach
    first = half * reach
    start = cols_ref[first, reach]
    place = jnp.int32(0)
    for e in range(reach):
        place = place + jnp.where(cols_ref[first, e] >= start, 1, 0)
    return cols_ref[first, reach - place + line % reach] - cols_ref[0, reach]


def halo_tile(cols_ref, odd, distance, reach, lags, outer):
    count = 2 * reach
    low_side = (odd == 0) if outer else (odd == 1)
    edge_line = 0 if outer else count - 1
    tile = own_tile(cols_ref, odd, edge_line, reach)
    lag = jnp.where(low_side, reach - 1 - distance, reach + 1 + distance)
    column = cols_ref[tile, lag]
    base = cols_ref[0, reach] + jnp.where(low_side, -reach, count)
    return jnp.clip(column - base, 0, reach - 1)


def near_kernel(
    odd_ref, cols_ref, cov_ref, std_ref, outer_ref, inner_ref, halo_ref,
    acc_ref, scale_ref, lag_ref, high_ref, low_ref, gram_ref, lags_ref, lines_ref,
    *, reach, lags, tile,
):
    odd = odd_ref[0]
    count = 2 * reach
    for e in range(lags):
        lags_ref[:, e * tile : (e + 1) * tile] = cov_ref[jnp.where(odd == 1, lags - 1 - e, e)]
    lag_ref[...] = lags_ref[:, : reach * tile]
    for line in range(3 * reach):
        if line < reach:
            index = own_tile(cols_ref, odd, line, reach) - jnp.where(odd == 1, reach, 0)
            source = outer_ref
        elif line < count:
            index = own_tile(cols_ref, odd, line, reach) - jnp.where(odd == 1, 0, reach)
            source = inner_ref
        else:
            index = halo_tile(cols_ref, odd, line - count, reach, lags, False)
            source = halo_ref
        place = pl.multiple_of(index * tile, tile)
        lines_ref[line * tile : (line + 1) * tile, :] = source[pl.ds(place, tile), :]
    for line in range(count):
        first = max(0, reach - line)
        start = max(0, line - reach) * tile
        product = jnp.dot(
            lags_ref[:, first * tile :],
            lines_ref[start : start + (lags - first) * tile, :],
            preferred_element_type=F32,
        )
        std = std_ref[pl.ds(own_tile(cols_ref, odd, line, reach), 1), :]
        if line < reach:
            rows = slice(line * tile, (line + 1) * tile)
            acc_ref[rows, :] = product
            scale_ref[rows, :] = as_column(std, LANES)
        else:
            rows = slice((line - reach) * tile, (line - reach + 1) * tile)
            high, low = split2(product * as_column(std, product.shape[1]))
            high_ref[rows, :] = high
            low_ref[rows, :] = low
    gram_ref[...] = rows_dot(
        high_ref[...], jnp.concatenate([high_ref[...], low_ref[...]], axis=1)
    )


def far_kernel(
    odd_ref, cols_ref, lag_ref, scale_ref, acc_ref, halo_ref, gram_ref,
    high_ref, low_ref, keep_ref, send_ref, lines_ref,
    *, reach, lags, tile, total,
):
    odd = odd_ref[0]
    width = acc_ref.shape[1]
    for line in range(reach):
        index = halo_tile(cols_ref, odd, reach - 1 - line, reach, lags, True)
        place = pl.multiple_of(index * tile, tile)
        lines_ref[line * tile : (line + 1) * tile, :] = halo_ref[pl.ds(place, tile), :]
    for line in range(reach):
        rows = slice(line * tile, (line + 1) * tile)
        product = acc_ref[rows, :] + jnp.dot(
            lag_ref[:, : (reach - line) * tile],
            lines_ref[line * tile :, :],
            preferred_element_type=F32,
        )
        scale = jnp.concatenate([scale_ref[rows, :]] * (width // LANES), axis=1)
        high, low = split2(product * scale)
        high_ref[rows, :] = high
        low_ref[rows, :] = low
    both = gram_ref[...] + rows_dot(
        high_ref[...], jnp.concatenate([high_ref[...], low_ref[...]], axis=1)
    )
    cross = both[:, width:]
    gram = (both[:, :width] + (cross + cross.T)) * (1.0 / total)
    half = width // 2
    packed = jnp.concatenate([gram[:half, :half], gram[:half, half:], gram[half:, half:]], axis=1)
    upper, lower = packed[: half // 2], packed[half // 2 :]
    keep_ref[...] = jnp.where(odd == 1, lower, upper)
    send_ref[...] = jnp.where(odd == 1, upper, lower)


def spread(value):
    return jnp.broadcast_to(value, (SUBLANES, LANES))


def eliminate(work_ref, factor_ref, inverse_ref, panel=32):
    size = work_ref.shape[0]
    groups = panel // SUBLANES
    sublane = lax.broadcasted_iota(jnp.int32, (SUBLANES, LANES), 0)
    lane = lax.broadcasted_iota(jnp.int32, (panel, size), 1)
    row = lax.broadcasted_iota(jnp.int32, (panel, size), 0)
    short_lane = lax.broadcasted_iota(jnp.int32, (panel, LANES), 1)
    short_row = lax.broadcasted_iota(jnp.int32, (panel, LANES), 0)
    chunks = range(0, size, LANES)
    for start in range(0, size, panel):
        stop = start + panel
        chunk = start // LANES * LANES
        offset = start - chunk
        block = work_ref[start:stop, :]
        identity = jnp.where(short_lane - offset == short_row, 1.0, 0.0).astype(F32)
        natural = [
            [block[i : i + SUBLANES, c : c + LANES] for c in chunks] + [identity[i : i + SUBLANES]]
            for i in range(0, panel, SUBLANES)
        ]
        corner = [natural[g][chunk // LANES] for g in range(groups)]
        columns = [
            {g: spread(corner[g][:, offset + k : offset + k + 1]) for g in range(k // SUBLANES, groups)}
            for k in range(panel)
        ]
        for k in range(panel):
            at, inside = divmod(k, SUBLANES)
            scale = lax.rsqrt(spread(columns[k][at][inside : inside + 1, :]))
            lower = {g: columns[k][g] * scale for g in range(at, groups)}
            for m in range(k + 1, panel):
                group, place = divmod(m, SUBLANES)
                factor = spread(lower[group][place : place + 1, :])
                for g in range(group, groups):
                    columns[m][g] = columns[m][g] - lower[g] * factor
            below = dict(lower)
            below[at] = jnp.where(sublane > inside, lower[at], 0.0)
            for c in range(len(natural[0])):
                pivot = spread(natural[at][c][inside : inside + 1, :]) * scale
                for g in range(at, groups):
                    natural[g][c] = natural[g][c] - below[g] * pivot
                natural[at][c] = jnp.where(sublane == inside, pivot, natural[at][c])
        done = jnp.concatenate([jnp.concatenate(v[:-1], axis=1) for v in natural], axis=0)
        inverse = jnp.concatenate([v[-1] for v in natural], axis=0)
        empty = jnp.zeros((panel, LANES), F32)
        inverse = jnp.concatenate([inverse if c == chunk else empty for c in chunks], axis=1)
        factor_ref[start:stop, :] = jnp.where(lane >= row + start, done, 0.0)
        inverse_ref[start:stop, :] = jnp.where(lane < start, done, inverse)
        if stop < size:
            own = (lane >= start) & (lane < stop)
            a, b, c = split3(done)
            x, y, z = split3(jnp.where(own, inverse, done))
            first = stop // LANES * LANES
            left = jnp.concatenate([a, a, b, a, c, b], axis=0)
            right = jnp.concatenate([x, y, x, z, x, y], axis=0)
            update = rows_dot(left[:, first:], right)
            rest = work_ref[stop:, :]
            rest_lane = lax.broadcasted_iota(jnp.int32, rest.shape, 1)
            rest = jnp.where((rest_lane >= start) & (rest_lane < stop), 0.0, rest)
            work_ref[stop:, :] = rest - update[stop - first :, :]


def basis_kernel(
    odd_ref, cols_ref, mine_ref, other_ref, far_high_ref, far_low_ref, near_high_ref, near_low_ref,
    basis_ref, factor_ref, work_ref, inverse_ref,
    *, reach, tile,
):
    odd = odd_ref[0]
    size = work_ref.shape[0]
    half = size // 2
    mine, other = mine_ref[...], other_ref[...]
    packed = jnp.concatenate(
        [jnp.where(odd == 1, other, mine), jnp.where(odd == 1, mine, other)], axis=0
    )
    corner = packed[:, half:size]
    work_ref[:half, :] = packed[:, :size]
    work_ref[half:, :half] = corner.T
    work_ref[half:, half:] = packed[:, size:]
    eliminate(work_ref, factor_ref, inverse_ref)
    high, low = split2(inverse_ref[...])
    right = jnp.concatenate([high, high, low], axis=1)
    for line in range(2 * reach):
        high_ref, low_ref = (far_high_ref, far_low_ref) if line < reach else (near_high_ref, near_low_ref)
        rows = slice(line % reach * tile, (line % reach + 1) * tile)
        left = jnp.concatenate([high_ref[rows, :], low_ref[rows, :], high_ref[rows, :]], axis=1)
        place = pl.multiple_of(own_tile(cols_ref, odd, line, reach) * tile, tile)
        basis_ref[pl.ds(place, tile), :] = lax.dot_general(
            left, right, (((1,), (1,)), ((), ())), preferred_element_type=F32
        )


def call(kernel, outs, scratch, smem_count, operands, flops, moved):
    in_specs = [
        pl.BlockSpec(memory_space=pltpu.SMEM if i < smem_count else pltpu.VMEM)
        for i in range(len(operands))
    ]
    return pl.pallas_call(
        kernel,
        out_shape=outs,
        in_specs=in_specs,
        out_specs=[pl.BlockSpec(memory_space=pltpu.VMEM) for _ in outs],
        scratch_shapes=scratch,
        cost_estimate=pl.CostEstimate(flops=flops, bytes_accessed=moved, transcendentals=0),
        compiler_params=pltpu.CompilerParams(vmem_limit_bytes=VMEM_LIMIT),
    )(*operands)


def per_device(device_count, sketch, marginal_std, cov_tiles, tile_cols):
    row_count, width = sketch.shape
    lags, tile, _ = cov_tiles.shape
    reach = (lags - 1) // 2
    halo = reach * tile
    assert row_count == 2 * halo and width % (2 * LANES) == 0
    assert device_count & (device_count - 1) == 0 and device_count > 1
    odd = lax.axis_index(AXES) % 2
    odd_arg = odd.astype(jnp.int32).reshape(1)

    def scaled(start):
        rows = lax.dynamic_slice_in_dim(sketch, start, halo, axis=0)
        std = lax.dynamic_slice_in_dim(marginal_std, start, halo, axis=0)
        return (rows.astype(F32) * std[:, None]).astype(BF16)

    def swap(value, mask):
        return lax.ppermute(value, AXES, [(i, i ^ mask) for i in range(device_count)])

    outer_pairs = []
    for i in range(1, device_count - 1, 2):
        outer_pairs += [(i, i + 1), (i + 1, i)]
    outer = scaled(jnp.where(odd == 1, halo, 0))
    inner = scaled(jnp.where(odd == 1, 0, halo))
    outer_halo = lax.ppermute(outer, AXES, outer_pairs)
    inner_halo = swap(inner, 1)

    def shape(rows, columns, dtype):
        return jax.ShapeDtypeStruct((rows, columns), dtype)

    acc, scale, lag_block, near_high, near_low, near_gram = call(
        functools.partial(near_kernel, reach=reach, lags=lags, tile=tile),
        [
            shape(halo, width, F32),
            shape(halo, LANES, F32),
            shape(tile, halo, BF16),
            shape(halo, width, BF16),
            shape(halo, width, BF16),
            shape(width, 2 * width, F32),
        ],
        [pltpu.VMEM((tile, lags * tile), BF16), pltpu.VMEM((3 * halo, width), BF16)],
        2,
        (odd_arg, tile_cols, cov_tiles, marginal_std.reshape(-1, tile), outer, inner, inner_halo),
        2 * 62 * tile * tile * width,
        8 << 20,
    )
    far_high, far_low, keep, send = call(
        functools.partial(
            far_kernel, reach=reach, lags=lags, tile=tile, total=row_count * device_count
        ),
        [
            shape(halo, width, BF16),
            shape(halo, width, BF16),
            shape(width // 4, width // 2 * 3, F32),
            shape(width // 4, width // 2 * 3, F32),
        ],
        [pltpu.VMEM((halo, width), BF16)],
        2,
        (odd_arg, tile_cols, lag_block, scale, acc, outer_halo, near_gram),
        2 * 18 * tile * tile * width,
        4 << 20,
    )
    gram = keep + swap(send, 1)
    mask = 2
    while mask < device_count:
        gram = gram + swap(gram, mask)
        mask *= 2
    other = swap(gram, 1)
    basis, factor = call(
        functools.partial(basis_kernel, reach=reach, tile=tile),
        [shape(row_count, width, F32), shape(width, width, F32)],
        [pltpu.VMEM((width, width), F32), pltpu.VMEM((width, width), F32)],
        2,
        (odd_arg, tile_cols, gram, other, far_high, far_low, near_high, near_low),
        2 * 24 * tile * tile * width,
        4 << 20,
    )
    return basis, factor


def solution(mesh):
    device_count = mesh.shape["grp"] * mesh.shape["dev"]
    in_specs = (P(AXES, None), P(AXES), P(), P(AXES, None))
    out_specs = (P(AXES, None), P())
    return jax.shard_map(
        functools.partial(per_device, device_count),
        mesh=mesh,
        in_specs=in_specs,
        out_specs=out_specs,
        check_vma=False,
    )
```

```python
import functools

import jax
import jax.numpy as jnp
from jax import lax
from jax.experimental import pallas as pl
from jax.experimental.pallas import tpu as pltpu
from jax.sharding import PartitionSpec as P

AXES = ("grp", "dev")
F32 = jnp.float32
BF16 = jnp.bfloat16
LANES = 128
SUBLANES = 8
VMEM_LIMIT = 48 * 1024 * 1024
SMALL_COST = pl.CostEstimate(flops=1, bytes_accessed=1, transcendentals=0)


def rows_dot(left, right):
    return lax.dot_general(left, right, (((0,), (0,)), ((), ())), preferred_element_type=F32)


def split2(value):
    high = value.astype(BF16)
    return high, (value - high.astype(F32)).astype(BF16)


def split3(value):
    high = value.astype(BF16)
    rest = value - high.astype(F32)
    middle = rest.astype(BF16)
    return high, middle, (rest - middle.astype(F32)).astype(BF16)


def std_column(std_ref, index, tile, width):
    rows = tile // LANES
    parts = [
        jnp.broadcast_to(std_ref[pl.ds(index * rows + i, 1), :], (LANES, LANES)).T for i in range(rows)
    ]
    column = jnp.concatenate(parts, axis=0)
    return jnp.concatenate([column] * (width // LANES), axis=1)


def own_tile(cols_ref, odd, line, reach):
    count = 2 * reach
    line = jnp.where(odd == 1, count - 1 - line, line)
    half = line // reach
    first = half * reach
    start = cols_ref[first, reach]
    place = jnp.int32(0)
    for e in range(reach):
        place = place + jnp.where(cols_ref[first, e] >= start, 1, 0)
    return cols_ref[first, reach - place + line % reach] - cols_ref[0, reach]


def halo_tile(cols_ref, odd, distance, reach, lags, outer):
    count = 2 * reach
    low_side = (odd == 0) if outer else (odd == 1)
    edge_line = 0 if outer else count - 1
    tile = own_tile(cols_ref, odd, edge_line, reach)
    lag = jnp.where(low_side, reach - 1 - distance, reach + 1 + distance)
    column = cols_ref[tile, lag]
    base = cols_ref[0, reach] + jnp.where(low_side, -reach, count)
    return jnp.clip(column - base, 0, reach - 1)


def scale_kernel(odd_ref, std_hbm_ref, sketch_ref, outer_ref, inner_ref, std_ref, rows_ref, sems, *, reach, tile):
    width = outer_ref.shape[1]
    count = 2 * reach
    first = jnp.where(odd_ref[0] == 1, reach, 0)
    order = [(first + i) % count for i in range(count)]
    copies = [pltpu.make_async_copy(std_hbm_ref, std_ref, sems.at[count])]
    for i, index in enumerate(order):
        place = pl.multiple_of(index * tile, tile)
        target = rows_ref.at[pl.ds(i * tile, tile), :]
        copies.append(pltpu.make_async_copy(sketch_ref.at[pl.ds(place, tile), :], target, sems.at[i]))
    for copy in copies:
        copy.start()
    copies[0].wait()
    for i, index in enumerate(order):
        std = std_column(std_ref, index, tile, width)
        copies[i + 1].wait()
        scaled = (rows_ref[i * tile : (i + 1) * tile, :].astype(F32) * std).astype(BF16)
        place = i % reach * tile
        (outer_ref if i < reach else inner_ref)[place : place + tile, :] = scaled


def near_kernel(
    odd_ref, cols_ref, cov_ref, std_ref, outer_ref, inner_ref, halo_ref,
    acc_ref, scale_ref, lag_ref, high_ref, low_ref, gram_ref, lags_ref, lines_ref,
    *, reach, lags, tile,
):
    odd = odd_ref[0]
    count = 2 * reach
    for e in range(lags):
        lags_ref[:, e * tile : (e + 1) * tile] = cov_ref[jnp.where(odd == 1, lags - 1 - e, e)]
    lag_ref[...] = lags_ref[:, : reach * tile]
    for line in range(3 * reach):
        if line < reach:
            index = own_tile(cols_ref, odd, line, reach) - jnp.where(odd == 1, reach, 0)
            source = outer_ref
        elif line < count:
            index = own_tile(cols_ref, odd, line, reach) - jnp.where(odd == 1, 0, reach)
            source = inner_ref
        else:
            index = halo_tile(cols_ref, odd, line - count, reach, lags, False)
            source = halo_ref
        place = pl.multiple_of(index * tile, tile)
        lines_ref[line * tile : (line + 1) * tile, :] = source[pl.ds(place, tile), :]
    for line in range(count):
        first = max(0, reach - line)
        start = max(0, line - reach) * tile
        product = jnp.dot(
            lags_ref[:, first * tile :],
            lines_ref[start : start + (lags - first) * tile, :],
            preferred_element_type=F32,
        )
        own = own_tile(cols_ref, odd, line, reach)
        if line < reach:
            rows = slice(line * tile, (line + 1) * tile)
            acc_ref[rows, :] = product
            scale_ref[rows, :] = std_column(std_ref, own, tile, LANES)
        else:
            rows = slice((line - reach) * tile, (line - reach + 1) * tile)
            high, low = split2(product * std_column(std_ref, own, tile, product.shape[1]))
            high_ref[rows, :] = high
            low_ref[rows, :] = low
    gram_ref[...] = rows_dot(
        high_ref[...], jnp.concatenate([high_ref[...], low_ref[...]], axis=1)
    )


def far_kernel(
    odd_ref, cols_ref, lag_ref, scale_ref, acc_ref, halo_ref, gram_ref,
    high_ref, low_ref, keep_ref, send_ref, lines_ref,
    *, reach, lags, tile, total,
):
    odd = odd_ref[0]
    width = acc_ref.shape[1]
    for line in range(reach):
        index = halo_tile(cols_ref, odd, reach - 1 - line, reach, lags, True)
        place = pl.multiple_of(index * tile, tile)
        lines_ref[line * tile : (line + 1) * tile, :] = halo_ref[pl.ds(place, tile), :]
    for line in range(reach):
        rows = slice(line * tile, (line + 1) * tile)
        product = acc_ref[rows, :] + jnp.dot(
            lag_ref[:, : (reach - line) * tile],
            lines_ref[line * tile :, :],
            preferred_element_type=F32,
        )
        scale = jnp.concatenate([scale_ref[rows, :]] * (width // LANES), axis=1)
        high, low = split2(product * scale)
        high_ref[rows, :] = high
        low_ref[rows, :] = low
    both = gram_ref[...] + rows_dot(
        high_ref[...], jnp.concatenate([high_ref[...], low_ref[...]], axis=1)
    )
    cross = both[:, width:]
    gram = (both[:, :width] + (cross + cross.T)) * (1.0 / total)
    packed = pack(gram)
    count = packed.shape[0] // 2
    upper, lower = packed[:count], packed[count:]
    keep_ref[...] = jnp.where(odd == 1, lower, upper)
    send_ref[...] = jnp.where(odd == 1, upper, lower)


def pack(gram):
    half = gram.shape[0] // 2
    row = lax.broadcasted_iota(jnp.int32, (half, half), 0)
    column = lax.broadcasted_iota(jnp.int32, (half, half), 1)
    last = gram[half:, half:]
    diagonal = jnp.sum(jnp.where(row == column, last, 0.0), axis=0, keepdims=True)
    extra = jnp.broadcast_to(diagonal, (SUBLANES, half))
    extra = jnp.concatenate([extra, extra], axis=1)
    body = jnp.concatenate([gram[:half, half:], jnp.where(column >= row, gram[:half, :half], last)], axis=1)
    return jnp.concatenate([body[: half // 2], extra, body[half // 2 :], extra], axis=0)


def unpack(upper, lower, work_ref):
    size = work_ref.shape[0]
    half = size // 2
    body = jnp.concatenate([upper[: half // 2], lower[: half // 2]], axis=0)
    corner, mixed = body[:, :half], body[:, half:]
    row = lax.broadcasted_iota(jnp.int32, (half, half), 0)
    column = lax.broadcasted_iota(jnp.int32, (half, half), 1)
    turned = mixed.T
    diagonal = jnp.broadcast_to(upper[half // 2 : half // 2 + 1, :half], (half, half))
    work_ref[:half, :half] = jnp.where(column >= row, mixed, turned)
    work_ref[:half, half:] = corner
    work_ref[half:, :half] = corner.T
    work_ref[half:, half:] = jnp.where(
        row == column, diagonal, jnp.where(column > row, turned, mixed)
    )


def spread(value):
    return jnp.broadcast_to(value, (SUBLANES, LANES))


def eliminate(work_ref, factor_ref, inverse_ref, panel=32):
    size = work_ref.shape[0]
    groups = panel // SUBLANES
    sublane = lax.broadcasted_iota(jnp.int32, (SUBLANES, LANES), 0)
    lane = lax.broadcasted_iota(jnp.int32, (panel, size), 1)
    row = lax.broadcasted_iota(jnp.int32, (panel, size), 0)
    short_lane = lax.broadcasted_iota(jnp.int32, (panel, LANES), 1)
    short_row = lax.broadcasted_iota(jnp.int32, (panel, LANES), 0)
    chunks = range(0, size, LANES)
    for start in range(0, size, panel):
        stop = start + panel
        chunk = start // LANES * LANES
        offset = start - chunk
        block = work_ref[start:stop, :]
        identity = jnp.where(short_lane - offset == short_row, 1.0, 0.0).astype(F32)
        natural = [
            [block[i : i + SUBLANES, c : c + LANES] for c in chunks] + [identity[i : i + SUBLANES]]
            for i in range(0, panel, SUBLANES)
        ]
        corner = [natural[g][chunk // LANES] for g in range(groups)]
        columns = [
            {g: spread(corner[g][:, offset + k : offset + k + 1]) for g in range(k // SUBLANES, groups)}
            for k in range(panel)
        ]
        for k in range(panel):
            at, inside = divmod(k, SUBLANES)
            scale = lax.rsqrt(spread(columns[k][at][inside : inside + 1, :]))
            lower = {g: columns[k][g] * scale for g in range(at, groups)}
            for m in range(k + 1, panel):
                group, place = divmod(m, SUBLANES)
                factor = spread(lower[group][place : place + 1, :])
                for g in range(group, groups):
                    columns[m][g] = columns[m][g] - lower[g] * factor
            below = dict(lower)
            below[at] = jnp.where(sublane > inside, lower[at], 0.0)
            for c in range(len(natural[0])):
                pivot = spread(natural[at][c][inside : inside + 1, :]) * scale
                for g in range(at, groups):
                    natural[g][c] = natural[g][c] - below[g] * pivot
                natural[at][c] = jnp.where(sublane == inside, pivot, natural[at][c])
        done = jnp.concatenate([jnp.concatenate(v[:-1], axis=1) for v in natural], axis=0)
        inverse = jnp.concatenate([v[-1] for v in natural], axis=0)
        empty = jnp.zeros((panel, LANES), F32)
        inverse = jnp.concatenate([inverse if c == chunk else empty for c in chunks], axis=1)
        factor_ref[start:stop, :] = jnp.where(lane >= row + start, done, 0.0)
        inverse_ref[start:stop, :] = jnp.where(lane < start, done, inverse)
        if stop < size:
            own = (lane >= start) & (lane < stop)
            a, b, c = split3(done)
            x, y, z = split3(jnp.where(own, inverse, done))
            first = stop // LANES * LANES
            left = jnp.concatenate([a, a, b, a, c, b], axis=0)
            right = jnp.concatenate([x, y, x, z, x, y], axis=0)
            update = rows_dot(left[:, first:], right)
            rest = work_ref[stop:, :]
            rest_lane = lax.broadcasted_iota(jnp.int32, rest.shape, 1)
            rest = jnp.where((rest_lane >= start) & (rest_lane < stop), 0.0, rest)
            work_ref[stop:, :] = rest - update[stop - first :, :]


def basis_kernel(
    odd_ref, cols_ref, mine_ref, other_ref, far_high_ref, far_low_ref, near_high_ref, near_low_ref,
    basis_ref, factor_ref, work_ref, inverse_ref,
    *, reach, tile,
):
    odd = odd_ref[0]
    mine, other = mine_ref[...], other_ref[...]
    unpack(jnp.where(odd == 1, other, mine), jnp.where(odd == 1, mine, other), work_ref)
    eliminate(work_ref, factor_ref, inverse_ref)
    high, low = split2(inverse_ref[...])
    right = jnp.concatenate([high, high, low], axis=1)
    for line in range(2 * reach):
        high_ref, low_ref = (far_high_ref, far_low_ref) if line < reach else (near_high_ref, near_low_ref)
        rows = slice(line % reach * tile, (line % reach + 1) * tile)
        left = jnp.concatenate([high_ref[rows, :], low_ref[rows, :], high_ref[rows, :]], axis=1)
        place = pl.multiple_of(own_tile(cols_ref, odd, line, reach) * tile, tile)
        basis_ref[pl.ds(place, tile), :] = lax.dot_general(
            left, right, (((1,), (1,)), ((), ())), preferred_element_type=F32
        )


def call(kernel, outs, scratch, smem_count, operands):
    in_specs = [
        pl.BlockSpec(memory_space=pltpu.SMEM if i < smem_count else pltpu.VMEM)
        for i in range(len(operands))
    ]
    return pl.pallas_call(
        kernel,
        out_shape=outs,
        in_specs=in_specs,
        out_specs=[pl.BlockSpec(memory_space=pltpu.VMEM) for _ in outs],
        scratch_shapes=scratch,
        cost_estimate=SMALL_COST,
        compiler_params=pltpu.CompilerParams(vmem_limit_bytes=VMEM_LIMIT),
    )(*operands)


def per_device(device_count, sketch, marginal_std, cov_tiles, tile_cols):
    row_count, width = sketch.shape
    lags, tile, _ = cov_tiles.shape
    reach = (lags - 1) // 2
    halo = reach * tile
    assert row_count == 2 * halo and width % (2 * LANES) == 0
    assert device_count & (device_count - 1) == 0 and device_count > 1
    odd = lax.axis_index(AXES) % 2
    odd_arg = odd.astype(jnp.int32).reshape(1)

    std_rows = marginal_std.reshape(-1, LANES)

    outer, inner = pl.pallas_call(
        functools.partial(scale_kernel, reach=reach, tile=tile),
        out_shape=[jax.ShapeDtypeStruct((halo, width), BF16)] * 2,
        in_specs=[
            pl.BlockSpec(memory_space=pltpu.SMEM),
            pl.BlockSpec(memory_space=pltpu.HBM),
            pl.BlockSpec(memory_space=pltpu.HBM),
        ],
        out_specs=[pl.BlockSpec(memory_space=pltpu.VMEM)] * 2,
        scratch_shapes=[
            pltpu.VMEM(std_rows.shape, F32),
            pltpu.VMEM((row_count, width), BF16),
            pltpu.SemaphoreType.DMA((2 * reach + 1,)),
        ],
        cost_estimate=SMALL_COST,
        compiler_params=pltpu.CompilerParams(vmem_limit_bytes=VMEM_LIMIT),
    )(
        odd_arg,
        pltpu.with_memory_space_constraint(std_rows, pltpu.HBM),
        pltpu.with_memory_space_constraint(sketch, pltpu.HBM),
    )

    def swap(value, mask):
        return lax.ppermute(value, AXES, [(i, i ^ mask) for i in range(device_count)])

    outer_pairs = []
    for i in range(1, device_count - 1, 2):
        outer_pairs += [(i, i + 1), (i + 1, i)]
    outer_halo = lax.ppermute(outer, AXES, outer_pairs)
    inner_halo = swap(inner, 1)

    def shape(rows, columns, dtype):
        return jax.ShapeDtypeStruct((rows, columns), dtype)

    acc, scale, lag_block, near_high, near_low, near_gram = call(
        functools.partial(near_kernel, reach=reach, lags=lags, tile=tile),
        [
            shape(halo, width, F32),
            shape(halo, LANES, F32),
            shape(tile, halo, BF16),
            shape(halo, width, BF16),
            shape(halo, width, BF16),
            shape(width, 2 * width, F32),
        ],
        [pltpu.VMEM((tile, lags * tile), BF16), pltpu.VMEM((3 * halo, width), BF16)],
        2,
        (odd_arg, tile_cols, cov_tiles, std_rows, outer, inner, inner_halo),
    )
    far_high, far_low, keep, send = call(
        functools.partial(
            far_kernel, reach=reach, lags=lags, tile=tile, total=row_count * device_count
        ),
        [
            shape(halo, width, BF16),
            shape(halo, width, BF16),
            shape(width // 4 + SUBLANES, width, F32),
            shape(width // 4 + SUBLANES, width, F32),
        ],
        [pltpu.VMEM((halo, width), BF16)],
        2,
        (odd_arg, tile_cols, lag_block, scale, acc, outer_halo, near_gram),
    )
    gram = keep + swap(send, 1)
    masks = [1 << i for i in range(1, device_count.bit_length() - 1)]
    middle = len(masks) // 2
    for even_mask, odd_mask in zip(masks[middle:] + masks[:middle], masks):
        pairs = [(i, i ^ (odd_mask if i % 2 else even_mask)) for i in range(device_count)]
        gram = gram + lax.ppermute(gram, AXES, pairs)
    other = swap(gram, 1)
    basis, factor = call(
        functools.partial(basis_kernel, reach=reach, tile=tile),
        [shape(row_count, width, F32), shape(width, width, F32)],
        [pltpu.VMEM((width, width), F32), pltpu.VMEM((width, width), F32)],
        2,
        (odd_arg, tile_cols, gram, other, far_high, far_low, near_high, near_low),
    )
    return basis, factor


def solution(mesh):
    device_count = mesh.shape["grp"] * mesh.shape["dev"]
    in_specs = (P(AXES, None), P(AXES), P(), P(AXES, None))
    out_specs = (P(AXES, None), P())
    return jax.shard_map(
        functools.partial(per_device, device_count),
        mesh=mesh,
        in_specs=in_specs,
        out_specs=out_specs,
        check_vma=False,
    )
```

```python
import functools

import jax
import jax.numpy as jnp
from jax import lax
from jax.experimental import pallas as pl
from jax.experimental.pallas import tpu as pltpu
from jax.sharding import PartitionSpec as P

AXES = ("grp", "dev")
F32 = jnp.float32
BF16 = jnp.bfloat16
LANES = 128
SUBLANES = 8
VMEM_LIMIT = 48 * 1024 * 1024
SMALL_COST = pl.CostEstimate(flops=1, bytes_accessed=1, transcendentals=0)


def rows_dot(left, right):
    return lax.dot_general(left, right, (((0,), (0,)), ((), ())), preferred_element_type=F32)


def split2(value):
    high = value.astype(BF16)
    return high, (value - high.astype(F32)).astype(BF16)


def split3(value):
    high = value.astype(BF16)
    rest = value - high.astype(F32)
    middle = rest.astype(BF16)
    return high, middle, (rest - middle.astype(F32)).astype(BF16)


def std_column(std_ref, index, tile, width):
    rows = tile // LANES
    parts = [
        jnp.broadcast_to(std_ref[pl.ds(index * rows + i, 1), :], (LANES, LANES)).T for i in range(rows)
    ]
    column = jnp.concatenate(parts, axis=0)
    return jnp.concatenate([column] * (width // LANES), axis=1)


def own_tile(cols_ref, odd, line, reach):
    count = 2 * reach
    line = jnp.where(odd == 1, count - 1 - line, line)
    half = line // reach
    first = half * reach
    start = cols_ref[first, reach]
    place = jnp.int32(0)
    for e in range(reach):
        place = place + jnp.where(cols_ref[first, e] >= start, 1, 0)
    return cols_ref[first, reach - place + line % reach] - cols_ref[0, reach]


def halo_tile(cols_ref, odd, distance, reach, lags, outer):
    count = 2 * reach
    low_side = (odd == 0) if outer else (odd == 1)
    edge_line = 0 if outer else count - 1
    tile = own_tile(cols_ref, odd, edge_line, reach)
    lag = jnp.where(low_side, reach - 1 - distance, reach + 1 + distance)
    column = cols_ref[tile, lag]
    base = cols_ref[0, reach] + jnp.where(low_side, -reach, count)
    return jnp.clip(column - base, 0, reach - 1)


def scale_kernel(odd_ref, std_hbm_ref, sketch_ref, outer_ref, inner_ref, std_ref, rows_ref, sems, *, reach, tile):
    width = outer_ref.shape[1]
    count = 2 * reach
    first = jnp.where(odd_ref[0] == 1, reach, 0)
    order = [(first + i) % count for i in range(count)]
    copies = [pltpu.make_async_copy(std_hbm_ref, std_ref, sems.at[count])]
    for i, index in enumerate(order):
        place = pl.multiple_of(index * tile, tile)
        target = rows_ref.at[pl.ds(i * tile, tile), :]
        copies.append(pltpu.make_async_copy(sketch_ref.at[pl.ds(place, tile), :], target, sems.at[i]))
    for copy in copies:
        copy.start()
    copies[0].wait()
    for i, index in enumerate(order):
        std = std_column(std_ref, index, tile, width)
        copies[i + 1].wait()
        scaled = (rows_ref[i * tile : (i + 1) * tile, :].astype(F32) * std).astype(BF16)
        place = i % reach * tile
        (outer_ref if i < reach else inner_ref)[place : place + tile, :] = scaled


def near_kernel(
    odd_ref, cols_ref, cov_ref, std_ref, outer_ref, inner_ref, halo_ref,
    acc_ref, scale_ref, lag_ref, high_ref, low_ref, gram_ref, lags_ref, lines_ref,
    *, reach, lags, tile,
):
    odd = odd_ref[0]
    count = 2 * reach
    for e in range(lags):
        lags_ref[:, e * tile : (e + 1) * tile] = cov_ref[jnp.where(odd == 1, lags - 1 - e, e)]
    lag_ref[...] = lags_ref[:, : reach * tile]
    for line in range(3 * reach):
        if line < reach:
            index = own_tile(cols_ref, odd, line, reach) - jnp.where(odd == 1, reach, 0)
            source = outer_ref
        elif line < count:
            index = own_tile(cols_ref, odd, line, reach) - jnp.where(odd == 1, 0, reach)
            source = inner_ref
        else:
            index = halo_tile(cols_ref, odd, line - count, reach, lags, False)
            source = halo_ref
        place = pl.multiple_of(index * tile, tile)
        lines_ref[line * tile : (line + 1) * tile, :] = source[pl.ds(place, tile), :]
    for line in range(count):
        first = max(0, reach - line)
        start = max(0, line - reach) * tile
        product = jnp.dot(
            lags_ref[:, first * tile :],
            lines_ref[start : start + (lags - first) * tile, :],
            preferred_element_type=F32,
        )
        own = own_tile(cols_ref, odd, line, reach)
        if line < reach:
            rows = slice(line * tile, (line + 1) * tile)
            acc_ref[rows, :] = product
            scale_ref[rows, :] = std_column(std_ref, own, tile, LANES)
        else:
            rows = slice((line - reach) * tile, (line - reach + 1) * tile)
            high, low = split2(product * std_column(std_ref, own, tile, product.shape[1]))
            high_ref[rows, :] = high
            low_ref[rows, :] = low
    gram_ref[...] = rows_dot(
        high_ref[...], jnp.concatenate([high_ref[...], low_ref[...]], axis=1)
    )


def far_kernel(
    odd_ref, cols_ref, lag_ref, scale_ref, acc_ref, halo_ref, gram_ref,
    high_ref, low_ref, keep_ref, send_ref, lines_ref,
    *, reach, lags, tile, total,
):
    odd = odd_ref[0]
    width = acc_ref.shape[1]
    for line in range(reach):
        index = halo_tile(cols_ref, odd, reach - 1 - line, reach, lags, True)
        place = pl.multiple_of(index * tile, tile)
        lines_ref[line * tile : (line + 1) * tile, :] = halo_ref[pl.ds(place, tile), :]
    for line in range(reach):
        rows = slice(line * tile, (line + 1) * tile)
        product = acc_ref[rows, :] + jnp.dot(
            lag_ref[:, : (reach - line) * tile],
            lines_ref[line * tile :, :],
            preferred_element_type=F32,
        )
        scale = jnp.concatenate([scale_ref[rows, :]] * (width // LANES), axis=1)
        high, low = split2(product * scale)
        high_ref[rows, :] = high
        low_ref[rows, :] = low
    both = gram_ref[...] + rows_dot(
        high_ref[...], jnp.concatenate([high_ref[...], low_ref[...]], axis=1)
    )
    cross = both[:, width:]
    gram = (both[:, :width] + (cross + cross.T)) * (1.0 / total)
    packed = pack(gram)
    count = packed.shape[0] // 2
    upper, lower = packed[:count], packed[count:]
    keep_ref[...] = jnp.where(odd == 1, lower, upper)
    send_ref[...] = jnp.where(odd == 1, upper, lower)


def pack(gram):
    half = gram.shape[0] // 2
    row = lax.broadcasted_iota(jnp.int32, (half, half), 0)
    column = lax.broadcasted_iota(jnp.int32, (half, half), 1)
    last = gram[half:, half:]
    diagonal = jnp.sum(jnp.where(row == column, last, 0.0), axis=0, keepdims=True)
    extra = jnp.broadcast_to(diagonal, (SUBLANES, half))
    extra = jnp.concatenate([extra, extra], axis=1)
    body = jnp.concatenate([gram[:half, half:], jnp.where(column >= row, gram[:half, :half], last)], axis=1)
    return jnp.concatenate([body[: half // 2], extra, body[half // 2 :], extra], axis=0)


def unpack(upper, lower, work_ref):
    size = work_ref.shape[0]
    half = size // 2
    body = jnp.concatenate([upper[: half // 2], lower[: half // 2]], axis=0)
    corner, mixed = body[:, :half], body[:, half:]
    row = lax.broadcasted_iota(jnp.int32, (half, half), 0)
    column = lax.broadcasted_iota(jnp.int32, (half, half), 1)
    turned = mixed.T
    diagonal = jnp.broadcast_to(upper[half // 2 : half // 2 + 1, :half], (half, half))
    work_ref[:half, :half] = jnp.where(column >= row, mixed, turned)
    work_ref[:half, half:] = corner
    work_ref[half:, :half] = corner.T
    work_ref[half:, half:] = jnp.where(
        row == column, diagonal, jnp.where(column > row, turned, mixed)
    )


def spread(value):
    return jnp.broadcast_to(value, (SUBLANES, LANES))


def eliminate(work_ref, factor_ref, inverse_ref, panel=32, held=16):
    size = work_ref.shape[0]
    groups = panel // SUBLANES
    sublane = lax.broadcasted_iota(jnp.int32, (SUBLANES, LANES), 0)
    lane = lax.broadcasted_iota(jnp.int32, (panel, size), 1)
    row = lax.broadcasted_iota(jnp.int32, (panel, size), 0)
    short_lane = lax.broadcasted_iota(jnp.int32, (panel, LANES), 1)
    short_row = lax.broadcasted_iota(jnp.int32, (panel, LANES), 0)
    chunks = range(0, size, LANES)
    for start in range(0, size, panel):
        stop = start + panel
        chunk = start // LANES * LANES
        offset = start - chunk
        block = work_ref[start:stop, :]
        identity = jnp.where(short_lane - offset == short_row, 1.0, 0.0).astype(F32)
        natural = [
            [block[i : i + SUBLANES, c : c + LANES] for c in chunks] + [identity[i : i + SUBLANES]]
            for i in range(0, panel, SUBLANES)
        ]
        for begin in range(0, panel, held):
            end = begin + held
            columns = {
                k: {
                    g: spread(natural[g][chunk // LANES][:, offset + k : offset + k + 1])
                    for g in range(k // SUBLANES, groups)
                }
                for k in range(begin, end)
            }
            pivot = None
            for k in range(begin, end):
                at, inside = divmod(k, SUBLANES)
                if pivot is None:
                    pivot = spread(columns[k][at][inside : inside + 1, :])
                inverse = 1.0 / pivot
                scale = lax.rsqrt(pivot)
                ratio = {g: columns[k][g] * inverse for g in range(at, groups)}
                if k + 1 < end:
                    group, place = divmod(k + 1, SUBLANES)
                    element = spread(columns[k][group][place : place + 1, :])
                    pivot = spread(columns[k + 1][group][place : place + 1, :]) - element * element * inverse
                for m in range(k + 1, end):
                    group, place = divmod(m, SUBLANES)
                    factor = spread(ratio[group][place : place + 1, :])
                    for g in range(group, groups):
                        columns[m][g] = columns[m][g] - columns[k][g] * factor
                below = dict(ratio)
                below[at] = jnp.where(sublane > inside, ratio[at], 0.0)
                for c in range(len(natural[0])):
                    raw = spread(natural[at][c][inside : inside + 1, :])
                    for g in range(at, groups):
                        natural[g][c] = natural[g][c] - below[g] * raw
                    natural[at][c] = jnp.where(sublane == inside, raw * scale, natural[at][c])
        done = jnp.concatenate([jnp.concatenate(v[:-1], axis=1) for v in natural], axis=0)
        inverse = jnp.concatenate([v[-1] for v in natural], axis=0)
        empty = jnp.zeros((panel, LANES), F32)
        inverse = jnp.concatenate([inverse if c == chunk else empty for c in chunks], axis=1)
        factor_ref[start:stop, :] = jnp.where(lane >= row + start, done, 0.0)
        inverse_ref[start:stop, :] = jnp.where(lane < start, done, inverse)
        if stop < size:
            own = (lane >= start) & (lane < stop)
            a, b, c = split3(done)
            x, y, z = split3(jnp.where(own, inverse, done))
            first = stop // LANES * LANES
            left = jnp.concatenate([a, a, b, a, c, b], axis=0)
            right = jnp.concatenate([x, y, x, z, x, y], axis=0)
            update = rows_dot(left[:, first:], right)
            rest = work_ref[stop:, :]
            rest_lane = lax.broadcasted_iota(jnp.int32, rest.shape, 1)
            rest = jnp.where((rest_lane >= start) & (rest_lane < stop), 0.0, rest)
            work_ref[stop:, :] = rest - update[stop - first :, :]


def basis_kernel(
    odd_ref, cols_ref, mine_ref, other_ref, far_high_ref, far_low_ref, near_high_ref, near_low_ref,
    basis_ref, factor_ref, work_ref, inverse_ref, tiles_ref, sems,
    *, reach, tile,
):
    odd = odd_ref[0]
    mine, other = mine_ref[...], other_ref[...]
    unpack(jnp.where(odd == 1, other, mine), jnp.where(odd == 1, mine, other), work_ref)
    eliminate(work_ref, factor_ref, inverse_ref)
    high, low = split2(inverse_ref[...])
    right = jnp.concatenate([high, high, low], axis=1)
    copies = []
    for line in range(2 * reach):
        high_ref, low_ref = (far_high_ref, far_low_ref) if line < reach else (near_high_ref, near_low_ref)
        rows = slice(line % reach * tile, (line % reach + 1) * tile)
        left = jnp.concatenate([high_ref[rows, :], low_ref[rows, :], high_ref[rows, :]], axis=1)
        tiles_ref[line] = lax.dot_general(
            left, right, (((1,), (1,)), ((), ())), preferred_element_type=F32
        )
        place = pl.multiple_of(own_tile(cols_ref, odd, line, reach) * tile, tile)
        copies.append(
            pltpu.make_async_copy(tiles_ref.at[line], basis_ref.at[pl.ds(place, tile), :], sems.at[line])
        )
        copies[-1].start()
    for copy in copies:
        copy.wait()


def call(kernel, outs, scratch, smem_count, operands, hbm_outs=0):
    in_specs = [
        pl.BlockSpec(memory_space=pltpu.SMEM if i < smem_count else pltpu.VMEM)
        for i in range(len(operands))
    ]
    return pl.pallas_call(
        kernel,
        out_shape=outs,
        in_specs=in_specs,
        out_specs=[
            pl.BlockSpec(memory_space=pl.ANY if i < hbm_outs else pltpu.VMEM) for i in range(len(outs))
        ],
        scratch_shapes=scratch,
        cost_estimate=SMALL_COST,
        compiler_params=pltpu.CompilerParams(vmem_limit_bytes=VMEM_LIMIT),
    )(*operands)


def per_device(device_count, sketch, marginal_std, cov_tiles, tile_cols):
    row_count, width = sketch.shape
    lags, tile, _ = cov_tiles.shape
    reach = (lags - 1) // 2
    halo = reach * tile
    assert row_count == 2 * halo and width % (2 * LANES) == 0
    assert device_count & (device_count - 1) == 0 and device_count > 1
    odd = lax.axis_index(AXES) % 2
    odd_arg = odd.astype(jnp.int32).reshape(1)

    std_rows = marginal_std.reshape(-1, LANES)

    outer, inner = pl.pallas_call(
        functools.partial(scale_kernel, reach=reach, tile=tile),
        out_shape=[jax.ShapeDtypeStruct((halo, width), BF16)] * 2,
        in_specs=[
            pl.BlockSpec(memory_space=pltpu.SMEM),
            pl.BlockSpec(memory_space=pltpu.HBM),
            pl.BlockSpec(memory_space=pltpu.HBM),
        ],
        out_specs=[pl.BlockSpec(memory_space=pltpu.VMEM)] * 2,
        scratch_shapes=[
            pltpu.VMEM(std_rows.shape, F32),
            pltpu.VMEM((row_count, width), BF16),
            pltpu.SemaphoreType.DMA((2 * reach + 1,)),
        ],
        cost_estimate=SMALL_COST,
        compiler_params=pltpu.CompilerParams(vmem_limit_bytes=VMEM_LIMIT),
    )(
        odd_arg,
        pltpu.with_memory_space_constraint(std_rows, pltpu.HBM),
        pltpu.with_memory_space_constraint(sketch, pltpu.HBM),
    )

    def swap(value, mask):
        return lax.ppermute(value, AXES, [(i, i ^ mask) for i in range(device_count)])

    outer_pairs = []
    for i in range(1, device_count - 1, 2):
        outer_pairs += [(i, i + 1), (i + 1, i)]
    outer_halo = lax.ppermute(outer, AXES, outer_pairs)
    inner_halo = swap(inner, 1)

    def shape(rows, columns, dtype):
        return jax.ShapeDtypeStruct((rows, columns), dtype)

    acc, scale, lag_block, near_high, near_low, near_gram = call(
        functools.partial(near_kernel, reach=reach, lags=lags, tile=tile),
        [
            shape(halo, width, F32),
            shape(halo, LANES, F32),
            shape(tile, halo, BF16),
            shape(halo, width, BF16),
            shape(halo, width, BF16),
            shape(width, 2 * width, F32),
        ],
        [pltpu.VMEM((tile, lags * tile), BF16), pltpu.VMEM((3 * halo, width), BF16)],
        2,
        (odd_arg, tile_cols, cov_tiles, std_rows, outer, inner, inner_halo),
    )
    far_high, far_low, keep, send = call(
        functools.partial(
            far_kernel, reach=reach, lags=lags, tile=tile, total=row_count * device_count
        ),
        [
            shape(halo, width, BF16),
            shape(halo, width, BF16),
            shape(width // 4 + SUBLANES, width, F32),
            shape(width // 4 + SUBLANES, width, F32),
        ],
        [pltpu.VMEM((halo, width), BF16)],
        2,
        (odd_arg, tile_cols, lag_block, scale, acc, outer_halo, near_gram),
    )
    gram = keep + swap(send, 1)
    bits = [1 << i for i in range(1, device_count.bit_length() - 1)]
    if len(bits) % 2:
        gram = gram + swap(gram, bits.pop())
    rounds = [(bits[i], bits[i + 1]) for i in range(0, len(bits), 2)]
    middle = len(rounds) // 2
    for even, odd_one in zip(rounds[middle:] + rounds[:middle], rounds):
        near, across, both = (
            lax.ppermute(
                gram, AXES, [(i, i ^ (odd_mask if i % 2 else even_mask)) for i in range(device_count)]
            )
            for even_mask, odd_mask in zip(
                (even[0], even[1], even[0] | even[1]), (odd_one[0], odd_one[1], odd_one[0] | odd_one[1])
            )
        )
        gram = (gram + near) + (across + both)
    other = swap(gram, 1)
    basis, factor = call(
        functools.partial(basis_kernel, reach=reach, tile=tile),
        [shape(row_count, width, F32), shape(width, width, F32)],
        [
            pltpu.VMEM((width, width), F32),
            pltpu.VMEM((width, width), F32),
            pltpu.VMEM((2 * reach, tile, width), F32),
            pltpu.SemaphoreType.DMA((2 * reach,)),
        ],
        2,
        (odd_arg, tile_cols, gram, other, far_high, far_low, near_high, near_low),
        1,
    )
    return basis, factor


def solution(mesh):
    device_count = mesh.shape["grp"] * mesh.shape["dev"]
    in_specs = (P(AXES, None), P(AXES), P(), P(AXES, None))
    out_specs = (P(AXES, None), P())
    return jax.shard_map(
        functools.partial(per_device, device_count),
        mesh=mesh,
        in_specs=in_specs,
        out_specs=out_specs,
        check_vma=False,
    )
```

```python
import functools

import jax
import jax.numpy as jnp
from jax import lax
from jax.experimental import pallas as pl
from jax.experimental.pallas import tpu as pltpu
from jax.sharding import PartitionSpec as P

AXES = ("grp", "dev")
F32 = jnp.float32
BF16 = jnp.bfloat16
LANES = 128
SUBLANES = 8
VMEM_LIMIT = 48 * 1024 * 1024
SMALL_COST = pl.CostEstimate(flops=1, bytes_accessed=1, transcendentals=0)


def rows_dot(left, right):
    return lax.dot_general(left, right, (((0,), (0,)), ((), ())), preferred_element_type=F32)


def split2(value):
    high = value.astype(BF16)
    return high, (value - high.astype(F32)).astype(BF16)


def split3(value):
    high = value.astype(BF16)
    rest = value - high.astype(F32)
    middle = rest.astype(BF16)
    return high, middle, (rest - middle.astype(F32)).astype(BF16)


def std_column(std_ref, index, tile, width):
    rows = tile // LANES
    parts = [
        jnp.broadcast_to(std_ref[pl.ds(index * rows + i, 1), :], (LANES, LANES)).T for i in range(rows)
    ]
    column = jnp.concatenate(parts, axis=0)
    return jnp.concatenate([column] * (width // LANES), axis=1)


def own_tile(cols_ref, odd, line, reach):
    count = 2 * reach
    line = jnp.where(odd == 1, count - 1 - line, line)
    half = line // reach
    first = half * reach
    start = cols_ref[first, reach]
    place = jnp.int32(0)
    for e in range(reach):
        place = place + jnp.where(cols_ref[first, e] >= start, 1, 0)
    return cols_ref[first, reach - place + line % reach] - cols_ref[0, reach]


def halo_tile(cols_ref, odd, distance, reach, lags, outer):
    count = 2 * reach
    low_side = (odd == 0) if outer else (odd == 1)
    edge_line = 0 if outer else count - 1
    tile = own_tile(cols_ref, odd, edge_line, reach)
    lag = jnp.where(low_side, reach - 1 - distance, reach + 1 + distance)
    column = cols_ref[tile, lag]
    base = cols_ref[0, reach] + jnp.where(low_side, -reach, count)
    return jnp.clip(column - base, 0, reach - 1)


def scale_kernel(first_ref, std_hbm_ref, sketch_ref, *refs, tile):
    out_ref, std_ref, rows_ref, sems = refs[-4:]
    count = out_ref.shape[0] // tile
    first = first_ref[0]
    copies = [pltpu.make_async_copy(std_hbm_ref, std_ref, sems.at[count])]
    for i in range(count):
        place = pl.multiple_of((first + i) * tile, tile)
        target = rows_ref.at[pl.ds(i * tile, tile), :]
        copies.append(pltpu.make_async_copy(sketch_ref.at[pl.ds(place, tile), :], target, sems.at[i]))
    for copy in copies:
        copy.start()
    copies[0].wait()
    for i in range(count):
        std = std_column(std_ref, first + i, tile, out_ref.shape[1])
        copies[i + 1].wait()
        rows = slice(i * tile, (i + 1) * tile)
        out_ref[rows, :] = (rows_ref[rows, :].astype(F32) * std).astype(BF16)


def near_kernel(
    odd_ref, cols_ref, cov_ref, std_ref, outer_ref, inner_ref, halo_ref,
    acc_ref, scale_ref, lag_ref, high_ref, low_ref, gram_ref, lags_ref, lines_ref,
    *, reach, lags, tile,
):
    odd = odd_ref[0]
    count = 2 * reach
    for e in range(lags):
        lags_ref[:, e * tile : (e + 1) * tile] = cov_ref[jnp.where(odd == 1, lags - 1 - e, e)]
    lag_ref[...] = lags_ref[:, : reach * tile]
    for line in range(3 * reach):
        if line < reach:
            index = own_tile(cols_ref, odd, line, reach) - jnp.where(odd == 1, reach, 0)
            source = outer_ref
        elif line < count:
            index = own_tile(cols_ref, odd, line, reach) - jnp.where(odd == 1, 0, reach)
            source = inner_ref
        else:
            index = halo_tile(cols_ref, odd, line - count, reach, lags, False)
            source = halo_ref
        place = pl.multiple_of(index * tile, tile)
        lines_ref[line * tile : (line + 1) * tile, :] = source[pl.ds(place, tile), :]
    for line in range(count):
        first = max(0, reach - line)
        start = max(0, line - reach) * tile
        product = jnp.dot(
            lags_ref[:, first * tile :],
            lines_ref[start : start + (lags - first) * tile, :],
            preferred_element_type=F32,
        )
        own = own_tile(cols_ref, odd, line, reach)
        if line < reach:
            rows = slice(line * tile, (line + 1) * tile)
            acc_ref[rows, :] = product
            scale_ref[rows, :] = std_column(std_ref, own, tile, LANES)
        else:
            rows = slice((line - reach) * tile, (line - reach + 1) * tile)
            high, low = split2(product * std_column(std_ref, own, tile, product.shape[1]))
            high_ref[rows, :] = high
            low_ref[rows, :] = low
    gram_ref[...] = rows_dot(
        high_ref[...], jnp.concatenate([high_ref[...], low_ref[...]], axis=1)
    )


def far_kernel(
    odd_ref, cols_ref, lag_ref, scale_ref, acc_ref, halo_ref, gram_ref,
    high_ref, low_ref, keep_ref, send_ref, lines_ref,
    *, reach, lags, tile, total,
):
    odd = odd_ref[0]
    width = acc_ref.shape[1]
    for line in range(reach):
        index = halo_tile(cols_ref, odd, reach - 1 - line, reach, lags, True)
        place = pl.multiple_of(index * tile, tile)
        lines_ref[line * tile : (line + 1) * tile, :] = halo_ref[pl.ds(place, tile), :]
    for line in range(reach):
        rows = slice(line * tile, (line + 1) * tile)
        product = acc_ref[rows, :] + jnp.dot(
            lag_ref[:, : (reach - line) * tile],
            lines_ref[line * tile :, :],
            preferred_element_type=F32,
        )
        scale = jnp.concatenate([scale_ref[rows, :]] * (width // LANES), axis=1)
        high, low = split2(product * scale)
        high_ref[rows, :] = high
        low_ref[rows, :] = low
    both = gram_ref[...] + rows_dot(
        high_ref[...], jnp.concatenate([high_ref[...], low_ref[...]], axis=1)
    )
    cross = both[:, width:]
    gram = (both[:, :width] + (cross + cross.T)) * (1.0 / total)
    packed = pack(gram)
    count = packed.shape[0] // 2
    upper, lower = packed[:count], packed[count:]
    keep_ref[...] = jnp.where(odd == 1, lower, upper)
    send_ref[...] = jnp.where(odd == 1, upper, lower)


def pack(gram):
    half = gram.shape[0] // 2
    row = lax.broadcasted_iota(jnp.int32, (half, half), 0)
    column = lax.broadcasted_iota(jnp.int32, (half, half), 1)
    last = gram[half:, half:]
    diagonal = jnp.sum(jnp.where(row == column, last, 0.0), axis=0, keepdims=True)
    extra = jnp.broadcast_to(diagonal, (SUBLANES, half))
    extra = jnp.concatenate([extra, extra], axis=1)
    body = jnp.concatenate([gram[:half, half:], jnp.where(column >= row, gram[:half, :half], last)], axis=1)
    return jnp.concatenate([body[: half // 2], extra, body[half // 2 :], extra], axis=0)


def unpack(upper, lower, work_ref):
    size = work_ref.shape[0]
    half = size // 2
    body = jnp.concatenate([upper[: half // 2], lower[: half // 2]], axis=0)
    corner, mixed = body[:, :half], body[:, half:]
    row = lax.broadcasted_iota(jnp.int32, (half, half), 0)
    column = lax.broadcasted_iota(jnp.int32, (half, half), 1)
    turned = mixed.T
    diagonal = jnp.broadcast_to(upper[half // 2 : half // 2 + 1, :half], (half, half))
    work_ref[:half, :half] = jnp.where(column >= row, mixed, turned)
    work_ref[:half, half:] = corner
    work_ref[half:, :half] = corner.T
    work_ref[half:, half:] = jnp.where(
        row == column, diagonal, jnp.where(column > row, turned, mixed)
    )


def spread(value):
    return jnp.broadcast_to(value, (SUBLANES, LANES))


def eliminate(work_ref, factor_ref, inverse_ref, panel=32, held=16):
    size = work_ref.shape[0]
    groups = panel // SUBLANES
    sublane = lax.broadcasted_iota(jnp.int32, (SUBLANES, LANES), 0)
    lane = lax.broadcasted_iota(jnp.int32, (panel, size), 1)
    row = lax.broadcasted_iota(jnp.int32, (panel, size), 0)
    short_lane = lax.broadcasted_iota(jnp.int32, (panel, LANES), 1)
    short_row = lax.broadcasted_iota(jnp.int32, (panel, LANES), 0)
    chunks = range(0, size, LANES)
    for start in range(0, size, panel):
        stop = start + panel
        chunk = start // LANES * LANES
        offset = start - chunk
        block = work_ref[start:stop, :]
        identity = jnp.where(short_lane - offset == short_row, 1.0, 0.0).astype(F32)
        natural = [
            [block[i : i + SUBLANES, c : c + LANES] for c in chunks] + [identity[i : i + SUBLANES]]
            for i in range(0, panel, SUBLANES)
        ]
        for begin in range(0, panel, held):
            end = begin + held
            columns = {
                k: {
                    g: spread(natural[g][chunk // LANES][:, offset + k : offset + k + 1])
                    for g in range(k // SUBLANES, groups)
                }
                for k in range(begin, end)
            }
            pivot = None
            for k in range(begin, end):
                at, inside = divmod(k, SUBLANES)
                if pivot is None:
                    pivot = spread(columns[k][at][inside : inside + 1, :])
                inverse = 1.0 / pivot
                scale = lax.rsqrt(pivot)
                ratio = {g: columns[k][g] * inverse for g in range(at, groups)}
                if k + 1 < end:
                    group, place = divmod(k + 1, SUBLANES)
                    element = spread(columns[k][group][place : place + 1, :])
                    pivot = spread(columns[k + 1][group][place : place + 1, :]) - element * element * inverse
                for m in range(k + 1, end):
                    group, place = divmod(m, SUBLANES)
                    factor = spread(ratio[group][place : place + 1, :])
                    for g in range(group, groups):
                        columns[m][g] = columns[m][g] - columns[k][g] * factor
                below = dict(ratio)
                below[at] = jnp.where(sublane > inside, ratio[at], 0.0)
                for c in range(len(natural[0])):
                    raw = spread(natural[at][c][inside : inside + 1, :])
                    for g in range(at, groups):
                        natural[g][c] = natural[g][c] - below[g] * raw
                    natural[at][c] = jnp.where(sublane == inside, raw * scale, natural[at][c])
        done = jnp.concatenate([jnp.concatenate(v[:-1], axis=1) for v in natural], axis=0)
        inverse = jnp.concatenate([v[-1] for v in natural], axis=0)
        empty = jnp.zeros((panel, LANES), F32)
        inverse = jnp.concatenate([inverse if c == chunk else empty for c in chunks], axis=1)
        factor_ref[start:stop, :] = jnp.where(lane >= row + start, done, 0.0)
        inverse_ref[start:stop, :] = jnp.where(lane < start, done, inverse)
        if stop < size:
            own = (lane >= start) & (lane < stop)
            a, b, c = split3(done)
            x, y, z = split3(jnp.where(own, inverse, done))
            first = stop // LANES * LANES
            left = jnp.concatenate([a, a, b, a, c, b], axis=0)
            right = jnp.concatenate([x, y, x, z, x, y], axis=0)
            update = rows_dot(left[:, first:], right)
            rest = work_ref[stop:, :]
            rest_lane = lax.broadcasted_iota(jnp.int32, rest.shape, 1)
            rest = jnp.where((rest_lane >= start) & (rest_lane < stop), 0.0, rest)
            work_ref[stop:, :] = rest - update[stop - first :, :]


def basis_kernel(
    odd_ref, cols_ref, mine_ref, other_ref, far_high_ref, far_low_ref, near_high_ref, near_low_ref,
    basis_ref, factor_ref, work_ref, inverse_ref, tiles_ref, held_ref, sems,
    *, reach, tile,
):
    odd = odd_ref[0]
    mine, other = mine_ref[...], other_ref[...]
    unpack(jnp.where(odd == 1, other, mine), jnp.where(odd == 1, mine, other), work_ref)
    eliminate(work_ref, held_ref, inverse_ref)
    factor_copy = pltpu.make_async_copy(held_ref, factor_ref, sems.at[2 * reach])
    factor_copy.start()
    high, low = split2(inverse_ref[...])
    right = jnp.concatenate([high, high, low], axis=1)
    copies = []
    for line in range(2 * reach):
        high_ref, low_ref = (far_high_ref, far_low_ref) if line < reach else (near_high_ref, near_low_ref)
        rows = slice(line % reach * tile, (line % reach + 1) * tile)
        left = jnp.concatenate([high_ref[rows, :], low_ref[rows, :], high_ref[rows, :]], axis=1)
        tiles_ref[line] = lax.dot_general(
            left, right, (((1,), (1,)), ((), ())), preferred_element_type=F32
        )
        place = pl.multiple_of(own_tile(cols_ref, odd, line, reach) * tile, tile)
        copies.append(
            pltpu.make_async_copy(tiles_ref.at[line], basis_ref.at[pl.ds(place, tile), :], sems.at[line])
        )
        copies[-1].start()
    for copy in copies:
        copy.wait()
    factor_copy.wait()


def call(kernel, outs, scratch, smem_count, operands, hbm_outs=0):
    in_specs = [
        pl.BlockSpec(memory_space=pltpu.SMEM if i < smem_count else pltpu.VMEM)
        for i in range(len(operands))
    ]
    return pl.pallas_call(
        kernel,
        out_shape=outs,
        in_specs=in_specs,
        out_specs=[
            pl.BlockSpec(memory_space=pl.ANY if i < hbm_outs else pltpu.VMEM) for i in range(len(outs))
        ],
        scratch_shapes=scratch,
        cost_estimate=SMALL_COST,
        compiler_params=pltpu.CompilerParams(vmem_limit_bytes=VMEM_LIMIT),
    )(*operands)


def per_device(device_count, sketch, marginal_std, cov_tiles, tile_cols):
    row_count, width = sketch.shape
    lags, tile, _ = cov_tiles.shape
    reach = (lags - 1) // 2
    halo = reach * tile
    assert row_count == 2 * halo and width % (2 * LANES) == 0
    assert device_count & (device_count - 1) == 0 and device_count > 1
    odd = lax.axis_index(AXES) % 2
    odd_arg = odd.astype(jnp.int32).reshape(1)

    std_rows = marginal_std.reshape(-1, LANES)

    def scaled(first, *after):
        return pl.pallas_call(
            functools.partial(scale_kernel, tile=tile),
            out_shape=jax.ShapeDtypeStruct((halo, width), BF16),
            in_specs=[
                pl.BlockSpec(memory_space=pltpu.SMEM),
                pl.BlockSpec(memory_space=pltpu.HBM),
                pl.BlockSpec(memory_space=pltpu.HBM),
            ]
            + [pl.BlockSpec(memory_space=pl.ANY)] * len(after),
            out_specs=pl.BlockSpec(memory_space=pltpu.VMEM),
            scratch_shapes=[
                pltpu.VMEM(std_rows.shape, F32),
                pltpu.VMEM((halo, width), BF16),
                pltpu.SemaphoreType.DMA((reach + 1,)),
            ],
            cost_estimate=SMALL_COST,
            compiler_params=pltpu.CompilerParams(vmem_limit_bytes=VMEM_LIMIT),
        )(
            first.astype(jnp.int32).reshape(1),
            pltpu.with_memory_space_constraint(std_rows, pltpu.HBM),
            pltpu.with_memory_space_constraint(sketch, pltpu.HBM),
            *after,
        )

    outer = scaled(jnp.where(odd == 1, reach, 0))
    inner = scaled(jnp.where(odd == 1, 0, reach), outer)

    def swap(value, mask):
        return lax.ppermute(value, AXES, [(i, i ^ mask) for i in range(device_count)])

    outer_pairs = []
    for i in range(1, device_count - 1, 2):
        outer_pairs += [(i, i + 1), (i + 1, i)]
    outer_halo = lax.ppermute(outer, AXES, outer_pairs)
    inner_halo = jnp.concatenate([swap(inner[: halo // 2], 1), swap(inner[halo // 2 :], 1)], axis=0)

    def shape(rows, columns, dtype):
        return jax.ShapeDtypeStruct((rows, columns), dtype)

    acc, scale, lag_block, near_high, near_low, near_gram = call(
        functools.partial(near_kernel, reach=reach, lags=lags, tile=tile),
        [
            shape(halo, width, F32),
            shape(halo, LANES, F32),
            shape(tile, halo, BF16),
            shape(halo, width, BF16),
            shape(halo, width, BF16),
            shape(width, 2 * width, F32),
        ],
        [pltpu.VMEM((tile, lags * tile), BF16), pltpu.VMEM((3 * halo, width), BF16)],
        2,
        (odd_arg, tile_cols, cov_tiles, std_rows, outer, inner, inner_halo),
    )
    far_high, far_low, keep, send = call(
        functools.partial(
            far_kernel, reach=reach, lags=lags, tile=tile, total=row_count * device_count
        ),
        [
            shape(halo, width, BF16),
            shape(halo, width, BF16),
            shape(width // 4 + SUBLANES, width, F32),
            shape(width // 4 + SUBLANES, width, F32),
        ],
        [pltpu.VMEM((halo, width), BF16)],
        2,
        (odd_arg, tile_cols, lag_block, scale, acc, outer_halo, near_gram),
    )
    gram = keep + swap(send, 1)
    bits = [1 << i for i in range(1, device_count.bit_length() - 1)]
    if len(bits) % 2:
        gram = gram + swap(gram, bits.pop())
    rounds = [(bits[i], bits[i + 1]) for i in range(0, len(bits), 2)]
    middle = len(rounds) // 2
    for even, odd_one in zip(rounds[middle:] + rounds[:middle], rounds):
        near, across, both = (
            lax.ppermute(
                gram, AXES, [(i, i ^ (odd_mask if i % 2 else even_mask)) for i in range(device_count)]
            )
            for even_mask, odd_mask in zip(
                (even[0], even[1], even[0] | even[1]), (odd_one[0], odd_one[1], odd_one[0] | odd_one[1])
            )
        )
        gram = (gram + near) + (across + both)
    other = swap(gram, 1)
    basis, factor = call(
        functools.partial(basis_kernel, reach=reach, tile=tile),
        [shape(row_count, width, F32), shape(width, width, F32)],
        [
            pltpu.VMEM((width, width), F32),
            pltpu.VMEM((width, width), F32),
            pltpu.VMEM((2 * reach, tile, width), F32),
            pltpu.VMEM((width, width), F32),
            pltpu.SemaphoreType.DMA((2 * reach + 1,)),
        ],
        2,
        (odd_arg, tile_cols, gram, other, far_high, far_low, near_high, near_low),
        2,
    )
    return basis, factor


def solution(mesh):
    device_count = mesh.shape["grp"] * mesh.shape["dev"]
    in_specs = (P(AXES, None), P(AXES), P(), P(AXES, None))
    out_specs = (P(AXES, None), P())
    return jax.shard_map(
        functools.partial(per_device, device_count),
        mesh=mesh,
        in_specs=in_specs,
        out_specs=out_specs,
        check_vma=False,
    )
```

```python
import functools

import jax
import jax.numpy as jnp
from jax import lax
from jax.experimental import pallas as pl
from jax.experimental.pallas import tpu as pltpu
from jax.sharding import PartitionSpec as P

AXES = ("grp", "dev")
F32 = jnp.float32
BF16 = jnp.bfloat16
LANES = 128
SUBLANES = 8
VMEM_LIMIT = 48 * 1024 * 1024
HALO_PARTS = 2
SMALL_COST = pl.CostEstimate(flops=1, bytes_accessed=1, transcendentals=0)


def rows_dot(left, right):
    return lax.dot_general(left, right, (((0,), (0,)), ((), ())), preferred_element_type=F32)


def split2(value):
    high = value.astype(BF16)
    return high, (value - high.astype(F32)).astype(BF16)


def split3(value):
    high = value.astype(BF16)
    rest = value - high.astype(F32)
    middle = rest.astype(BF16)
    return high, middle, (rest - middle.astype(F32)).astype(BF16)


def std_column(std_ref, index, tile, width):
    rows = tile // LANES
    parts = [
        jnp.broadcast_to(std_ref[pl.ds(index * rows + i, 1), :], (LANES, LANES)).T for i in range(rows)
    ]
    column = jnp.concatenate(parts, axis=0)
    return jnp.concatenate([column] * (width // LANES), axis=1)


def own_tile(cols_ref, odd, line, reach):
    count = 2 * reach
    line = jnp.where(odd == 1, count - 1 - line, line)
    half = line // reach
    first = half * reach
    start = cols_ref[first, reach]
    place = jnp.int32(0)
    for e in range(reach):
        place = place + jnp.where(cols_ref[first, e] >= start, 1, 0)
    return cols_ref[first, reach - place + line % reach] - cols_ref[0, reach]


def odd_device():
    return lax.rem(lax.axis_index(AXES), 2)


def scale_kernel(cols_hbm_ref, std_hbm_ref, sketch_ref, *refs, reach, tile, inner):
    out_ref, cols_ref, std_ref, rows_ref, sems = refs[-5:]
    odd = odd_device()
    first = jnp.where(odd == (0 if inner else 1), reach, 0)
    place = pl.multiple_of(first * tile, tile)
    copies = [
        pltpu.make_async_copy(sketch_ref.at[pl.ds(place, reach * tile), :], rows_ref, sems.at[0]),
        pltpu.make_async_copy(cols_hbm_ref, cols_ref, sems.at[1]),
        pltpu.make_async_copy(std_hbm_ref, std_ref, sems.at[2]),
    ]
    for copy in copies:
        copy.start()
    copies[1].wait()
    copies[2].wait()
    tiles = [own_tile(cols_ref, odd, line + (reach if inner else 0), reach) for line in range(reach)]
    columns = [std_column(std_ref, index, tile, out_ref.shape[1]) for index in tiles]
    copies[0].wait()
    for line in range(reach):
        place = pl.multiple_of((tiles[line] - first) * tile, tile)
        rows = rows_ref[pl.ds(place, tile), :].astype(F32)
        out_ref[line * tile : (line + 1) * tile, :] = (rows * columns[line]).astype(BF16)


def near_kernel(
    cols_ref, cov_ref, std_ref, outer_ref, inner_ref, *refs, reach, lags, tile
):
    halo_refs = refs[:HALO_PARTS]
    acc_ref, scale_ref, lag_ref, high_ref, low_ref, gram_ref, lags_ref, lines_ref = refs[HALO_PARTS:]
    odd = odd_device()
    count = 2 * reach
    for e in range(lags):
        lags_ref[:, e * tile : (e + 1) * tile] = cov_ref[jnp.where(odd == 1, lags - 1 - e, e)]
    for e in range(reach):
        lag_ref[:, e * tile : (e + 1) * tile] = lags_ref[:, (reach - 1 - e) * tile : (reach - e) * tile]
    half = reach * tile
    lines_ref[:half, :] = outer_ref[...]
    lines_ref[half : 2 * half, :] = inner_ref[...]
    part = half // HALO_PARTS
    for line in range(reach):
        place = (reach - 1 - line) * tile
        source = halo_refs[place // part]
        lines_ref[2 * half + line * tile : 2 * half + (line + 1) * tile, :] = source[
            place % part : place % part + tile, :
        ]
    for line in range(count):
        first = max(0, reach - line)
        start = max(0, line - reach) * tile
        product = jnp.dot(
            lags_ref[:, first * tile :],
            lines_ref[start : start + (lags - first) * tile, :],
            preferred_element_type=F32,
        )
        own = own_tile(cols_ref, odd, line, reach)
        if line < reach:
            rows = slice(line * tile, (line + 1) * tile)
            acc_ref[rows, :] = product
            scale_ref[rows, :] = std_column(std_ref, own, tile, LANES)
        else:
            rows = slice((line - reach) * tile, (line - reach + 1) * tile)
            high, low = split2(product * std_column(std_ref, own, tile, product.shape[1]))
            high_ref[rows, :] = high
            low_ref[rows, :] = low
    gram_ref[...] = rows_dot(
        high_ref[...], jnp.concatenate([high_ref[...], low_ref[...]], axis=1)
    )


def far_kernel(
    lag_ref, scale_ref, acc_ref, halo_ref, gram_ref, high_ref, low_ref, keep_ref, send_ref,
    *, reach, tile, total,
):
    odd = odd_device()
    width = acc_ref.shape[1]
    for line in range(reach):
        rows = slice(line * tile, (line + 1) * tile)
        product = acc_ref[rows, :] + jnp.dot(
            lag_ref[:, line * tile :],
            halo_ref[: (reach - line) * tile, :],
            preferred_element_type=F32,
        )
        scale = jnp.concatenate([scale_ref[rows, :]] * (width // LANES), axis=1)
        high, low = split2(product * scale)
        high_ref[rows, :] = high
        low_ref[rows, :] = low
    both = gram_ref[...] + rows_dot(
        high_ref[...], jnp.concatenate([high_ref[...], low_ref[...]], axis=1)
    )
    cross = both[:, width:]
    gram = (both[:, :width] + (cross + cross.T)) * (1.0 / total)
    packed = pack(gram)
    count = packed.shape[0] // 2
    upper, lower = packed[:count], packed[count:]
    keep_ref[...] = jnp.where(odd == 1, lower, upper)
    send_ref[...] = jnp.where(odd == 1, upper, lower)


def pack(gram):
    half = gram.shape[0] // 2
    row = lax.broadcasted_iota(jnp.int32, (half, half), 0)
    column = lax.broadcasted_iota(jnp.int32, (half, half), 1)
    last = gram[half:, half:]
    diagonal = jnp.sum(jnp.where(row == column, last, 0.0), axis=0, keepdims=True)
    extra = jnp.broadcast_to(diagonal, (SUBLANES, half))
    extra = jnp.concatenate([extra, extra], axis=1)
    body = jnp.concatenate([gram[:half, half:], jnp.where(column >= row, gram[:half, :half], last)], axis=1)
    return jnp.concatenate([body[: half // 2], extra, body[half // 2 :], extra], axis=0)


def unpack(upper, lower, work_ref):
    size = work_ref.shape[0]
    half = size // 2
    body = jnp.concatenate([upper[: half // 2], lower[: half // 2]], axis=0)
    corner, mixed = body[:, :half], body[:, half:]
    row = lax.broadcasted_iota(jnp.int32, (half, half), 0)
    column = lax.broadcasted_iota(jnp.int32, (half, half), 1)
    turned = mixed.T
    diagonal = jnp.broadcast_to(upper[half // 2 : half // 2 + 1, :half], (half, half))
    work_ref[:half, :half] = jnp.where(column >= row, mixed, turned)
    work_ref[:half, half:] = corner
    work_ref[half:, :half] = corner.T
    work_ref[half:, half:] = jnp.where(
        row == column, diagonal, jnp.where(column > row, turned, mixed)
    )


def spread(value):
    return jnp.broadcast_to(value, (SUBLANES, LANES))


def eliminate(work_ref, factor_ref, inverse_ref, panel=32, held=16):
    size = work_ref.shape[0]
    groups = panel // SUBLANES
    sublane = lax.broadcasted_iota(jnp.int32, (SUBLANES, LANES), 0)
    lane = lax.broadcasted_iota(jnp.int32, (panel, size), 1)
    row = lax.broadcasted_iota(jnp.int32, (panel, size), 0)
    short_lane = lax.broadcasted_iota(jnp.int32, (panel, LANES), 1)
    short_row = lax.broadcasted_iota(jnp.int32, (panel, LANES), 0)
    chunks = range(0, size, LANES)
    for start in range(0, size, panel):
        stop = start + panel
        chunk = start // LANES * LANES
        offset = start - chunk
        block = work_ref[start:stop, :]
        identity = jnp.where(short_lane - offset == short_row, 1.0, 0.0).astype(F32)
        natural = [
            [block[i : i + SUBLANES, c : c + LANES] for c in chunks] + [identity[i : i + SUBLANES]]
            for i in range(0, panel, SUBLANES)
        ]
        for begin in range(0, panel, held):
            end = begin + held
            columns = {
                k: {
                    g: spread(natural[g][chunk // LANES][:, offset + k : offset + k + 1])
                    for g in range(k // SUBLANES, groups)
                }
                for k in range(begin, end)
            }
            pivot = None
            for k in range(begin, end):
                at, inside = divmod(k, SUBLANES)
                if pivot is None:
                    pivot = spread(columns[k][at][inside : inside + 1, :])
                inverse = 1.0 / pivot
                scale = lax.rsqrt(pivot)
                ratio = {g: columns[k][g] * inverse for g in range(at, groups)}
                if k + 1 < end:
                    group, place = divmod(k + 1, SUBLANES)
                    element = spread(columns[k][group][place : place + 1, :])
                    pivot = spread(columns[k + 1][group][place : place + 1, :]) - element * element * inverse
                for m in range(k + 1, end):
                    group, place = divmod(m, SUBLANES)
                    factor = spread(ratio[group][place : place + 1, :])
                    for g in range(group, groups):
                        columns[m][g] = columns[m][g] - columns[k][g] * factor
                below = dict(ratio)
                below[at] = jnp.where(sublane > inside, ratio[at], 0.0)
                for c in range(len(natural[0])):
                    raw = spread(natural[at][c][inside : inside + 1, :])
                    for g in range(at, groups):
                        natural[g][c] = natural[g][c] - below[g] * raw
                    natural[at][c] = jnp.where(sublane == inside, raw * scale, natural[at][c])
        done = jnp.concatenate([jnp.concatenate(v[:-1], axis=1) for v in natural], axis=0)
        inverse = jnp.concatenate([v[-1] for v in natural], axis=0)
        empty = jnp.zeros((panel, LANES), F32)
        inverse = jnp.concatenate([inverse if c == chunk else empty for c in chunks], axis=1)
        factor_ref[start:stop, :] = jnp.where(lane >= row + start, done, 0.0)
        inverse_ref[start:stop, :] = jnp.where(lane < start, done, inverse)
        if stop < size:
            own = (lane >= start) & (lane < stop)
            a, b, c = split3(done)
            x, y, z = split3(jnp.where(own, inverse, done))
            first = stop // LANES * LANES
            left = jnp.concatenate([a, a, b, a, c, b], axis=0)
            right = jnp.concatenate([x, y, x, z, x, y], axis=0)
            update = rows_dot(left[:, first:], right)
            rest = work_ref[stop:, :]
            rest_lane = lax.broadcasted_iota(jnp.int32, rest.shape, 1)
            rest = jnp.where((rest_lane >= start) & (rest_lane < stop), 0.0, rest)
            work_ref[stop:, :] = rest - update[stop - first :, :]


def basis_kernel(
    cols_hbm_ref, mine_ref, other_ref, far_high_ref, far_low_ref, near_high_ref, near_low_ref,
    basis_ref, factor_ref, work_ref, inverse_ref, tiles_ref, held_ref, cols_ref, sems,
    *, reach, tile,
):
    odd = odd_device()
    cols_copy = pltpu.make_async_copy(cols_hbm_ref, cols_ref, sems.at[2 * reach + 1])
    cols_copy.start()
    mine, other = mine_ref[...], other_ref[...]
    unpack(jnp.where(odd == 1, other, mine), jnp.where(odd == 1, mine, other), work_ref)
    eliminate(work_ref, held_ref, inverse_ref)
    factor_copy = pltpu.make_async_copy(held_ref, factor_ref, sems.at[2 * reach])
    factor_copy.start()
    cols_copy.wait()
    high, low = split2(inverse_ref[...])
    right = jnp.concatenate([high, high, low], axis=1)
    copies = []
    for line in range(2 * reach):
        high_ref, low_ref = (far_high_ref, far_low_ref) if line < reach else (near_high_ref, near_low_ref)
        rows = slice(line % reach * tile, (line % reach + 1) * tile)
        left = jnp.concatenate([high_ref[rows, :], low_ref[rows, :], high_ref[rows, :]], axis=1)
        tiles_ref[line] = lax.dot_general(
            left, right, (((1,), (1,)), ((), ())), preferred_element_type=F32
        )
        place = pl.multiple_of(own_tile(cols_ref, odd, line, reach) * tile, tile)
        copies.append(
            pltpu.make_async_copy(tiles_ref.at[line], basis_ref.at[pl.ds(place, tile), :], sems.at[line])
        )
        copies[-1].start()
    for copy in copies:
        copy.wait()
    factor_copy.wait()


def call(kernel, outs, scratch, spaces, operands, out_spaces=None):
    operands = [
        pltpu.with_memory_space_constraint(operand, space) if space is pltpu.HBM else operand
        for operand, space in zip(operands, spaces)
    ]
    return pl.pallas_call(
        kernel,
        out_shape=outs,
        in_specs=[pl.BlockSpec(memory_space=space) for space in spaces],
        out_specs=[pl.BlockSpec(memory_space=space) for space in out_spaces or [pltpu.VMEM] * len(outs)],
        scratch_shapes=scratch,
        cost_estimate=SMALL_COST,
        compiler_params=pltpu.CompilerParams(vmem_limit_bytes=VMEM_LIMIT),
    )(*operands)


def per_device(device_count, sketch, marginal_std, cov_tiles, tile_cols):
    row_count, width = sketch.shape
    lags, tile, _ = cov_tiles.shape
    reach = (lags - 1) // 2
    halo = reach * tile
    assert row_count == 2 * halo and width % (2 * LANES) == 0
    assert device_count & (device_count - 1) == 0 and device_count > 1
    def swap(value, mask):
        return lax.ppermute(value, AXES, [(i, i ^ mask) for i in range(device_count)])

    outer_pairs = []
    for i in range(1, device_count - 1, 2):
        outer_pairs += [(i, i + 1), (i + 1, i)]
    std_rows = marginal_std.reshape(-1, LANES)

    def shape(rows, columns, dtype):
        return jax.ShapeDtypeStruct((rows, columns), dtype)

    def scaled(inner, *after):
        return call(
            functools.partial(scale_kernel, reach=reach, tile=tile, inner=inner),
            [shape(halo, width, BF16)],
            [
                pltpu.SMEM(tile_cols.shape, jnp.int32),
                pltpu.VMEM(std_rows.shape, F32),
                pltpu.VMEM((halo, width), BF16),
                pltpu.SemaphoreType.DMA((3,)),
            ],
            [pltpu.HBM] * 3 + [pl.ANY] * len(after),
            (tile_cols, std_rows, sketch, *after),
        )[0]

    outer = scaled(False)
    inner = scaled(True, outer)
    outer_halo = lax.ppermute(outer, AXES, outer_pairs)
    part = halo // HALO_PARTS
    inner_halo = [swap(inner[i : i + part], 1) for i in range(0, halo, part)]
    acc, scale, lag_block, near_high, near_low, near_gram = call(
        functools.partial(near_kernel, reach=reach, lags=lags, tile=tile),
        [
            shape(halo, width, F32),
            shape(halo, LANES, F32),
            shape(tile, halo, BF16),
            shape(halo, width, BF16),
            shape(halo, width, BF16),
            shape(width, 2 * width, F32),
        ],
        [pltpu.VMEM((tile, lags * tile), BF16), pltpu.VMEM((3 * halo, width), BF16)],
        [pltpu.SMEM] + [pltpu.VMEM] * (4 + HALO_PARTS),
        (tile_cols, cov_tiles, std_rows, outer, inner, *inner_halo),
    )
    far_high, far_low, keep, send = call(
        functools.partial(far_kernel, reach=reach, tile=tile, total=row_count * device_count),
        [
            shape(halo, width, BF16),
            shape(halo, width, BF16),
            shape(width // 4 + SUBLANES, width, F32),
            shape(width // 4 + SUBLANES, width, F32),
        ],
        [],
        [pltpu.VMEM] * 5,
        (lag_block, scale, acc, outer_halo, near_gram),
    )
    gram = keep + swap(send, 1)
    bits = [1 << i for i in range(1, device_count.bit_length() - 1)]
    if len(bits) % 2:
        gram = gram + swap(gram, bits.pop())
    rounds = [(bits[i], bits[i + 1]) for i in range(0, len(bits), 2)]
    middle = len(rounds) // 2
    for even, odd_one in zip(rounds[middle:] + rounds[:middle], rounds):
        near, across, both = (
            lax.ppermute(
                gram, AXES, [(i, i ^ (odd_mask if i % 2 else even_mask)) for i in range(device_count)]
            )
            for even_mask, odd_mask in zip(
                (even[0], even[1], even[0] | even[1]), (odd_one[0], odd_one[1], odd_one[0] | odd_one[1])
            )
        )
        gram = (gram + near) + (across + both)
    other = swap(gram, 1)
    basis, factor = call(
        functools.partial(basis_kernel, reach=reach, tile=tile),
        [shape(row_count, width, F32), shape(width, width, F32)],
        [
            pltpu.VMEM((width, width), F32),
            pltpu.VMEM((width, width), F32),
            pltpu.VMEM((2 * reach, tile, width), F32),
            pltpu.VMEM((width, width), F32),
            pltpu.SMEM(tile_cols.shape, jnp.int32),
            pltpu.SemaphoreType.DMA((2 * reach + 2,)),
        ],
        [pltpu.HBM] + [pltpu.VMEM] * 6,
        (tile_cols, gram, other, far_high, far_low, near_high, near_low),
        [pl.ANY] * 2,
    )
    return basis, factor


def solution(mesh):
    device_count = mesh.shape["grp"] * mesh.shape["dev"]
    in_specs = (P(AXES, None), P(AXES), P(), P(AXES, None))
    out_specs = (P(AXES, None), P())
    return jax.shard_map(
        functools.partial(per_device, device_count),
        mesh=mesh,
        in_specs=in_specs,
        out_specs=out_specs,
        check_vma=False,
    )
```

```python
import functools

import jax
import jax.numpy as jnp
from jax import lax
from jax.experimental import pallas as pl
from jax.experimental.pallas import tpu as pltpu
from jax.sharding import PartitionSpec as P

AXES = ("grp", "dev")
F32 = jnp.float32
BF16 = jnp.bfloat16
LANES = 128
SUBLANES = 8
VMEM_LIMIT = 48 * 1024 * 1024
HALO_PARTS = 2
SMALL_COST = pl.CostEstimate(flops=1, bytes_accessed=1, transcendentals=0)


def rows_dot(left, right):
    return lax.dot_general(left, right, (((0,), (0,)), ((), ())), preferred_element_type=F32)


def split2(value):
    high = value.astype(BF16)
    return high, (value - high.astype(F32)).astype(BF16)


def split3(value):
    high = value.astype(BF16)
    rest = value - high.astype(F32)
    middle = rest.astype(BF16)
    return high, middle, (rest - middle.astype(F32)).astype(BF16)


def std_column(std_ref, index, tile, width):
    rows = tile // LANES
    parts = [
        jnp.broadcast_to(std_ref[pl.ds(index * rows + i, 1), :], (LANES, LANES)).T for i in range(rows)
    ]
    column = jnp.concatenate(parts, axis=0)
    return jnp.concatenate([column] * (width // LANES), axis=1)


def own_tile(cols_ref, odd, line, reach):
    count = 2 * reach
    line = jnp.where(odd == 1, count - 1 - line, line)
    half = line // reach
    first = half * reach
    start = cols_ref[first, reach]
    place = jnp.int32(0)
    for e in range(reach):
        place = place + jnp.where(cols_ref[first, e] >= start, 1, 0)
    return cols_ref[first, reach - place + line % reach] - cols_ref[0, reach]


def odd_device():
    return lax.rem(lax.axis_index(AXES), 2)


def scale_kernel(cols_hbm_ref, std_hbm_ref, sketch_ref, *refs, reach, tile, inner):
    out_ref, cols_ref, std_ref, rows_ref, sems = refs[-5:]
    odd = odd_device()
    first = jnp.where(odd == (0 if inner else 1), reach, 0)
    cols_copy = pltpu.make_async_copy(cols_hbm_ref, cols_ref, sems.at[reach])
    std_copy = pltpu.make_async_copy(std_hbm_ref, std_ref, sems.at[reach + 1])
    copies = []
    for i in range(reach):
        place = pl.multiple_of((first + i) * tile, tile)
        target = rows_ref.at[pl.ds(i * tile, tile), :]
        copies.append(pltpu.make_async_copy(sketch_ref.at[pl.ds(place, tile), :], target, sems.at[i]))
    for copy in (std_copy, cols_copy, *copies):
        copy.start()
    std_copy.wait()
    columns = [std_column(std_ref, first + i, tile, out_ref.shape[1]) for i in range(reach)]
    cols_copy.wait()
    for i in range(reach):
        line = jnp.int32(0)
        for e in range(reach):
            line = line + jnp.where(cols_ref[first + i, e] >= cols_ref[first, reach], 1, 0)
        line = jnp.where(odd == 1, reach - 1 - line, line)
        copies[i].wait()
        place = pl.multiple_of(line * tile, tile)
        rows = rows_ref[i * tile : (i + 1) * tile, :].astype(F32)
        out_ref[pl.ds(place, tile), :] = (rows * columns[i]).astype(BF16)


def near_kernel(
    cols_ref, cov_ref, std_ref, outer_ref, inner_ref, *refs, reach, lags, tile
):
    halo_refs = refs[:HALO_PARTS]
    acc_ref, scale_ref, lag_ref, high_ref, low_ref, gram_ref, lags_ref, lines_ref = refs[HALO_PARTS:]
    odd = odd_device()
    count = 2 * reach
    for e in range(lags):
        lags_ref[:, e * tile : (e + 1) * tile] = cov_ref[jnp.where(odd == 1, lags - 1 - e, e)]
    for e in range(reach):
        lag_ref[:, e * tile : (e + 1) * tile] = lags_ref[:, (reach - 1 - e) * tile : (reach - e) * tile]
    half = reach * tile
    lines_ref[:half, :] = outer_ref[...]
    lines_ref[half : 2 * half, :] = inner_ref[...]
    part = half // HALO_PARTS
    for line in range(reach):
        place = (reach - 1 - line) * tile
        source = halo_refs[place // part]
        lines_ref[2 * half + line * tile : 2 * half + (line + 1) * tile, :] = source[
            place % part : place % part + tile, :
        ]
    for line in range(count):
        first = max(0, reach - line)
        start = max(0, line - reach) * tile
        product = jnp.dot(
            lags_ref[:, first * tile :],
            lines_ref[start : start + (lags - first) * tile, :],
            preferred_element_type=F32,
        )
        own = own_tile(cols_ref, odd, line, reach)
        if line < reach:
            rows = slice(line * tile, (line + 1) * tile)
            acc_ref[rows, :] = product
            scale_ref[rows, :] = std_column(std_ref, own, tile, LANES)
        else:
            rows = slice((line - reach) * tile, (line - reach + 1) * tile)
            high, low = split2(product * std_column(std_ref, own, tile, product.shape[1]))
            high_ref[rows, :] = high
            low_ref[rows, :] = low
    gram_ref[...] = rows_dot(
        high_ref[...], jnp.concatenate([high_ref[...], low_ref[...]], axis=1)
    )


def far_kernel(
    lag_ref, scale_ref, acc_ref, halo_ref, gram_ref, high_ref, low_ref, keep_ref, send_ref,
    *, reach, tile, total,
):
    odd = odd_device()
    width = acc_ref.shape[1]
    for line in range(reach):
        rows = slice(line * tile, (line + 1) * tile)
        product = acc_ref[rows, :] + jnp.dot(
            lag_ref[:, line * tile :],
            halo_ref[: (reach - line) * tile, :],
            preferred_element_type=F32,
        )
        scale = jnp.concatenate([scale_ref[rows, :]] * (width // LANES), axis=1)
        high, low = split2(product * scale)
        high_ref[rows, :] = high
        low_ref[rows, :] = low
    both = gram_ref[...] + rows_dot(
        high_ref[...], jnp.concatenate([high_ref[...], low_ref[...]], axis=1)
    )
    cross = both[:, width:]
    gram = (both[:, :width] + (cross + cross.T)) * (1.0 / total)
    packed = pack(gram)
    count = packed.shape[0] // 2
    upper, lower = packed[:count], packed[count:]
    keep_ref[...] = jnp.where(odd == 1, lower, upper)
    send_ref[...] = jnp.where(odd == 1, upper, lower)


def pack(gram):
    half = gram.shape[0] // 2
    row = lax.broadcasted_iota(jnp.int32, (half, half), 0)
    column = lax.broadcasted_iota(jnp.int32, (half, half), 1)
    last = gram[half:, half:]
    diagonal = jnp.sum(jnp.where(row == column, last, 0.0), axis=0, keepdims=True)
    extra = jnp.broadcast_to(diagonal, (SUBLANES, half))
    extra = jnp.concatenate([extra, extra], axis=1)
    body = jnp.concatenate([gram[:half, half:], jnp.where(column >= row, gram[:half, :half], last)], axis=1)
    return jnp.concatenate([body[: half // 2], extra, body[half // 2 :], extra], axis=0)


def unpack(upper, lower, work_ref):
    size = work_ref.shape[0]
    half = size // 2
    body = jnp.concatenate([upper[: half // 2], lower[: half // 2]], axis=0)
    corner, mixed = body[:, :half], body[:, half:]
    row = lax.broadcasted_iota(jnp.int32, (half, half), 0)
    column = lax.broadcasted_iota(jnp.int32, (half, half), 1)
    turned = mixed.T
    diagonal = jnp.broadcast_to(upper[half // 2 : half // 2 + 1, :half], (half, half))
    work_ref[:half, :half] = jnp.where(column >= row, mixed, turned)
    work_ref[:half, half:] = corner
    work_ref[half:, :half] = corner.T
    work_ref[half:, half:] = jnp.where(
        row == column, diagonal, jnp.where(column > row, turned, mixed)
    )


def spread(value):
    return jnp.broadcast_to(value, (SUBLANES, LANES))


def eliminate(work_ref, factor_ref, inverse_ref, panel=32, ahead=12, step=4):
    size = work_ref.shape[0]
    groups = panel // SUBLANES
    sublane = lax.broadcasted_iota(jnp.int32, (SUBLANES, LANES), 0)
    lane = lax.broadcasted_iota(jnp.int32, (SUBLANES, LANES), 1)
    wide_lane = lax.broadcasted_iota(jnp.int32, (panel, size), 1)
    chunks = range(0, size, LANES)
    for start in range(0, size, panel):
        stop = start + panel
        chunk = start // LANES * LANES
        at_chunk = chunk // LANES
        offset = start - chunk
        block = work_ref[start:stop, :]
        natural = [
            [block[i : i + SUBLANES, c : c + LANES] for c in chunks] for i in range(0, panel, SUBLANES)
        ]
        lower = [jnp.zeros((SUBLANES, LANES), F32) for _ in range(groups)]
        scale_row = jnp.zeros((SUBLANES, LANES), F32)
        scale_column = [jnp.zeros((SUBLANES, LANES), F32) for _ in range(groups)]
        columns = {}

        def keep(count):
            begin, end = len(columns), len(columns) + count
            for k in range(begin, end):
                columns[k] = {
                    g: spread(natural[g][at_chunk][:, offset + k : offset + k + 1])
                    for g in range(k // SUBLANES, groups)
                }
            kept = (lane >= offset + begin) & (lane < offset + end)
            for g in range(groups):
                identity = jnp.where(lane - offset == sublane + g * SUBLANES, 1.0, 0.0).astype(F32)
                natural[g][at_chunk] = jnp.where(kept, identity, natural[g][at_chunk])

        keep(ahead)
        pivot = spread(columns[0][0][:1, :])
        for k in range(panel):
            at, inside = divmod(k, SUBLANES)
            inverse = 1.0 / pivot
            scale = lax.rsqrt(pivot)
            ratio = {g: columns[k][g] * inverse for g in range(at, groups)}
            if k + 1 < panel:
                group, place = divmod(k + 1, SUBLANES)
                element = spread(columns[k][group][place : place + 1, :])
                pivot = spread(columns[k + 1][group][place : place + 1, :]) - element * element * inverse
            for m in range(k + 1, len(columns)):
                group, place = divmod(m, SUBLANES)
                factor = spread(ratio[group][place : place + 1, :])
                for g in range(group, groups):
                    columns[m][g] = columns[m][g] - columns[k][g] * factor
            below = dict(ratio)
            below[at] = jnp.where(sublane > inside, ratio[at], 0.0)
            for c in range(len(natural[0])):
                raw = spread(natural[at][c][inside : inside + 1, :])
                for g in range(at, groups):
                    natural[g][c] = natural[g][c] - below[g] * raw
            for g in range(at, groups):
                lower[g] = jnp.where(lane == offset + k, columns[k][g], lower[g])
            scale_row = jnp.where(lane == offset + k, scale, scale_row)
            scale_column[at] = jnp.where(sublane == inside, scale, scale_column[at])
            if (k + 1) % step == 0 and len(columns) < panel:
                keep(step)
        done = jnp.concatenate(
            [jnp.concatenate([v * scale_column[g] for v in natural[g]], axis=1) for g in range(groups)], axis=0
        )
        if stop < size:
            a, b, c = split3(done)
            left = jnp.concatenate([a, a, b, a, c, b], axis=0)
            right = jnp.concatenate([a, b, a, c, a, b], axis=0)
            first = stop // LANES * LANES
            update = rows_dot(left[:, first:], right)
            rest = work_ref[stop:, :]
            rest_lane = lax.broadcasted_iota(jnp.int32, rest.shape, 1)
            rest = jnp.where((rest_lane >= start) & (rest_lane < stop), 0.0, rest)
            work_ref[stop:, :] = rest - update[stop - first :, :]
        corner = jnp.concatenate([v * scale_row for v in lower], axis=0)
        row = lax.broadcasted_iota(jnp.int32, corner.shape, 0)
        short_lane = lax.broadcasted_iota(jnp.int32, corner.shape, 1)
        corner = jnp.where(short_lane <= row + offset, corner, 0.0)
        parts = [jnp.zeros((offset, LANES), F32), corner, jnp.zeros((LANES - offset - panel, LANES), F32)]
        turned = jnp.concatenate([v for v in parts if v.shape[0]], axis=0).T[offset : offset + panel]
        empty = jnp.zeros((panel, LANES), F32)
        turned = jnp.concatenate([turned if c == chunk else empty for c in chunks], axis=1)
        factor_ref[start:stop, :] = jnp.where(wide_lane >= stop, done, turned)
        inverse_ref[start:stop, :] = jnp.where(wide_lane < stop, done, 0.0)


def basis_kernel(
    cols_hbm_ref, mine_ref, other_ref, far_high_ref, far_low_ref, near_high_ref, near_low_ref,
    basis_ref, factor_ref, work_ref, inverse_ref, tiles_ref, held_ref, cols_ref, sems,
    *, reach, tile,
):
    odd = odd_device()
    cols_copy = pltpu.make_async_copy(cols_hbm_ref, cols_ref, sems.at[2 * reach + 1])
    cols_copy.start()
    mine, other = mine_ref[...], other_ref[...]
    unpack(jnp.where(odd == 1, other, mine), jnp.where(odd == 1, mine, other), work_ref)
    eliminate(work_ref, held_ref, inverse_ref)
    factor_copy = pltpu.make_async_copy(held_ref, factor_ref, sems.at[2 * reach])
    factor_copy.start()
    cols_copy.wait()
    high, low = split2(inverse_ref[...])
    right = jnp.concatenate([high, high, low], axis=1)
    copies = []
    for line in range(2 * reach):
        high_ref, low_ref = (far_high_ref, far_low_ref) if line < reach else (near_high_ref, near_low_ref)
        rows = slice(line % reach * tile, (line % reach + 1) * tile)
        left = jnp.concatenate([high_ref[rows, :], low_ref[rows, :], high_ref[rows, :]], axis=1)
        tiles_ref[line] = lax.dot_general(
            left, right, (((1,), (1,)), ((), ())), preferred_element_type=F32
        )
        place = pl.multiple_of(own_tile(cols_ref, odd, line, reach) * tile, tile)
        copies.append(
            pltpu.make_async_copy(tiles_ref.at[line], basis_ref.at[pl.ds(place, tile), :], sems.at[line])
        )
        copies[-1].start()
    for copy in copies:
        copy.wait()
    factor_copy.wait()


def call(kernel, outs, scratch, spaces, operands, out_spaces=None):
    operands = [
        pltpu.with_memory_space_constraint(operand, space) if space is pltpu.HBM else operand
        for operand, space in zip(operands, spaces)
    ]
    return pl.pallas_call(
        kernel,
        out_shape=outs,
        in_specs=[pl.BlockSpec(memory_space=space) for space in spaces],
        out_specs=[pl.BlockSpec(memory_space=space) for space in out_spaces or [pltpu.VMEM] * len(outs)],
        scratch_shapes=scratch,
        cost_estimate=SMALL_COST,
        compiler_params=pltpu.CompilerParams(vmem_limit_bytes=VMEM_LIMIT),
    )(*operands)


def per_device(device_count, sketch, marginal_std, cov_tiles, tile_cols):
    row_count, width = sketch.shape
    lags, tile, _ = cov_tiles.shape
    reach = (lags - 1) // 2
    halo = reach * tile
    assert row_count == 2 * halo and width % (2 * LANES) == 0
    assert device_count & (device_count - 1) == 0 and device_count > 1
    def swap(value, mask):
        return lax.ppermute(value, AXES, [(i, i ^ mask) for i in range(device_count)])

    outer_pairs = []
    for i in range(1, device_count - 1, 2):
        outer_pairs += [(i, i + 1), (i + 1, i)]
    std_rows = marginal_std.reshape(-1, LANES)

    def shape(rows, columns, dtype):
        return jax.ShapeDtypeStruct((rows, columns), dtype)

    def scaled(inner, *after):
        return call(
            functools.partial(scale_kernel, reach=reach, tile=tile, inner=inner),
            [shape(halo, width, BF16)],
            [
                pltpu.SMEM(tile_cols.shape, jnp.int32),
                pltpu.VMEM(std_rows.shape, F32),
                pltpu.VMEM((halo, width), BF16),
                pltpu.SemaphoreType.DMA((reach + 2,)),
            ],
            [pltpu.HBM] * 3 + [pl.ANY] * len(after),
            (tile_cols, std_rows, sketch, *after),
        )[0]

    outer = scaled(False)
    inner = scaled(True, outer)
    outer_halo = lax.ppermute(outer, AXES, outer_pairs)
    part = halo // HALO_PARTS
    inner_halo = [swap(inner[i : i + part], 1) for i in range(0, halo, part)]
    acc, scale, lag_block, near_high, near_low, near_gram = call(
        functools.partial(near_kernel, reach=reach, lags=lags, tile=tile),
        [
            shape(halo, width, F32),
            shape(halo, LANES, F32),
            shape(tile, halo, BF16),
            shape(halo, width, BF16),
            shape(halo, width, BF16),
            shape(width, 2 * width, F32),
        ],
        [pltpu.VMEM((tile, lags * tile), BF16), pltpu.VMEM((3 * halo, width), BF16)],
        [pltpu.SMEM] + [pltpu.VMEM] * (4 + HALO_PARTS),
        (tile_cols, cov_tiles, std_rows, outer, inner, *inner_halo),
    )
    far_high, far_low, keep, send = call(
        functools.partial(far_kernel, reach=reach, tile=tile, total=row_count * device_count),
        [
            shape(halo, width, BF16),
            shape(halo, width, BF16),
            shape(width // 4 + SUBLANES, width, F32),
            shape(width // 4 + SUBLANES, width, F32),
        ],
        [],
        [pltpu.VMEM] * 5,
        (lag_block, scale, acc, outer_halo, near_gram),
    )
    gram = keep + swap(send, 1)
    bits = [1 << i for i in range(1, device_count.bit_length() - 1)]
    if len(bits) % 2:
        gram = gram + swap(gram, bits.pop())
    rounds = [(bits[i], bits[i + 1]) for i in range(0, len(bits), 2)]
    middle = len(rounds) // 2
    for even, odd_one in zip(rounds[middle:] + rounds[:middle], rounds):
        near, across, both = (
            lax.ppermute(
                gram, AXES, [(i, i ^ (odd_mask if i % 2 else even_mask)) for i in range(device_count)]
            )
            for even_mask, odd_mask in zip(
                (even[0], even[1], even[0] | even[1]), (odd_one[0], odd_one[1], odd_one[0] | odd_one[1])
            )
        )
        gram = (gram + near) + (across + both)
    other = swap(gram, 1)
    basis, factor = call(
        functools.partial(basis_kernel, reach=reach, tile=tile),
        [shape(row_count, width, F32), shape(width, width, F32)],
        [
            pltpu.VMEM((width, width), F32),
            pltpu.VMEM((width, width), F32),
            pltpu.VMEM((2 * reach, tile, width), F32),
            pltpu.VMEM((width, width), F32),
            pltpu.SMEM(tile_cols.shape, jnp.int32),
            pltpu.SemaphoreType.DMA((2 * reach + 2,)),
        ],
        [pltpu.HBM] + [pltpu.VMEM] * 6,
        (tile_cols, gram, other, far_high, far_low, near_high, near_low),
        [pl.ANY] * 2,
    )
    return basis, factor


def solution(mesh):
    device_count = mesh.shape["grp"] * mesh.shape["dev"]
    in_specs = (P(AXES, None), P(AXES), P(), P(AXES, None))
    out_specs = (P(AXES, None), P())
    return jax.shard_map(
        functools.partial(per_device, device_count),
        mesh=mesh,
        in_specs=in_specs,
        out_specs=out_specs,
        check_vma=False,
    )
```

```python
import functools

import jax
import jax.numpy as jnp
from jax import lax
from jax.experimental import pallas as pl
from jax.experimental.pallas import tpu as pltpu
from jax.sharding import PartitionSpec as P

AXES = ("grp", "dev")
F32 = jnp.float32
BF16 = jnp.bfloat16
LANES = 128
SUBLANES = 8
VMEM_LIMIT = 48 * 1024 * 1024
HALO_PARTS = 2
SMALL_COST = pl.CostEstimate(flops=1, bytes_accessed=1, transcendentals=0)


def rows_dot(left, right):
    return lax.dot_general(left, right, (((0,), (0,)), ((), ())), preferred_element_type=F32)


def split2(value):
    high = value.astype(BF16)
    return high, (value - high.astype(F32)).astype(BF16)


def split3(value):
    high = value.astype(BF16)
    rest = value - high.astype(F32)
    middle = rest.astype(BF16)
    return high, middle, (rest - middle.astype(F32)).astype(BF16)


def std_column(std_ref, index, tile, width):
    rows = tile // LANES
    parts = [
        jnp.broadcast_to(std_ref[pl.ds(index * rows + i, 1), :], (LANES, LANES)).T for i in range(rows)
    ]
    column = jnp.concatenate(parts, axis=0)
    return jnp.concatenate([column] * (width // LANES), axis=1)


def own_tile(cols_ref, odd, line, reach):
    count = 2 * reach
    line = jnp.where(odd == 1, count - 1 - line, line)
    half = line // reach
    first = half * reach
    start = cols_ref[first, reach]
    place = jnp.int32(0)
    for e in range(reach):
        place = place + jnp.where(cols_ref[first, e] >= start, 1, 0)
    return cols_ref[first, reach - place + line % reach] - cols_ref[0, reach]


def odd_device():
    return lax.rem(lax.axis_index(AXES), 2)


def scale_kernel(cols_hbm_ref, std_hbm_ref, sketch_ref, *refs, reach, tile, inner):
    out_ref, cols_ref, std_ref, rows_ref, sems = refs[-5:]
    odd = odd_device()
    first = jnp.where(odd == (0 if inner else 1), reach, 0)
    cols_copy = pltpu.make_async_copy(cols_hbm_ref, cols_ref, sems.at[reach])
    std_copy = pltpu.make_async_copy(std_hbm_ref, std_ref, sems.at[reach + 1])
    copies = []
    for i in range(reach):
        place = pl.multiple_of((first + i) * tile, tile)
        target = rows_ref.at[pl.ds(i * tile, tile), :]
        copies.append(pltpu.make_async_copy(sketch_ref.at[pl.ds(place, tile), :], target, sems.at[i]))
    for copy in (std_copy, cols_copy, *copies):
        copy.start()
    std_copy.wait()
    columns = [std_column(std_ref, first + i, tile, out_ref.shape[1]) for i in range(reach)]
    cols_copy.wait()
    for i in range(reach):
        line = jnp.int32(0)
        for e in range(reach):
            line = line + jnp.where(cols_ref[first + i, e] >= cols_ref[first, reach], 1, 0)
        line = jnp.where(odd == 1, reach - 1 - line, line)
        copies[i].wait()
        place = pl.multiple_of(line * tile, tile)
        rows = rows_ref[i * tile : (i + 1) * tile, :].astype(F32)
        out_ref[pl.ds(place, tile), :] = (rows * columns[i]).astype(BF16)


def near_kernel(
    cols_ref, cov_ref, std_ref, outer_ref, inner_ref, *refs, reach, lags, tile
):
    halo_refs = refs[:HALO_PARTS]
    acc_ref, scale_ref, lag_ref, high_ref, low_ref, gram_ref, lags_ref, lines_ref = refs[HALO_PARTS:]
    odd = odd_device()
    count = 2 * reach
    for e in range(lags):
        lags_ref[:, e * tile : (e + 1) * tile] = cov_ref[jnp.where(odd == 1, lags - 1 - e, e)]
    for e in range(reach):
        lag_ref[:, e * tile : (e + 1) * tile] = lags_ref[:, (reach - 1 - e) * tile : (reach - e) * tile]
    half = reach * tile
    lines_ref[:half, :] = outer_ref[...]
    lines_ref[half : 2 * half, :] = inner_ref[...]
    part = half // HALO_PARTS
    for line in range(reach):
        place = (reach - 1 - line) * tile
        source = halo_refs[place // part]
        lines_ref[2 * half + line * tile : 2 * half + (line + 1) * tile, :] = source[
            place % part : place % part + tile, :
        ]
    for line in range(count):
        first = max(0, reach - line)
        start = max(0, line - reach) * tile
        product = jnp.dot(
            lags_ref[:, first * tile :],
            lines_ref[start : start + (lags - first) * tile, :],
            preferred_element_type=F32,
        )
        own = own_tile(cols_ref, odd, line, reach)
        if line < reach:
            rows = slice(line * tile, (line + 1) * tile)
            acc_ref[rows, :] = product
            scale_ref[rows, :] = std_column(std_ref, own, tile, LANES)
        else:
            rows = slice((line - reach) * tile, (line - reach + 1) * tile)
            high, low = split2(product * std_column(std_ref, own, tile, product.shape[1]))
            high_ref[rows, :] = high
            low_ref[rows, :] = low
    gram_ref[...] = rows_dot(
        high_ref[...], jnp.concatenate([high_ref[...], low_ref[...]], axis=1)
    )


def far_kernel(
    lag_ref, scale_ref, acc_ref, halo_ref, gram_ref, high_ref, low_ref, keep_ref, send_ref,
    *, reach, tile, total,
):
    odd = odd_device()
    width = acc_ref.shape[1]
    for line in range(reach):
        rows = slice(line * tile, (line + 1) * tile)
        product = acc_ref[rows, :] + jnp.dot(
            lag_ref[:, line * tile :],
            halo_ref[: (reach - line) * tile, :],
            preferred_element_type=F32,
        )
        scale = jnp.concatenate([scale_ref[rows, :]] * (width // LANES), axis=1)
        high, low = split2(product * scale)
        high_ref[rows, :] = high
        low_ref[rows, :] = low
    both = gram_ref[...] + rows_dot(
        high_ref[...], jnp.concatenate([high_ref[...], low_ref[...]], axis=1)
    )
    cross = both[:, width:]
    gram = (both[:, :width] + (cross + cross.T)) * (1.0 / total)
    packed = pack(gram)
    count = packed.shape[0] // 2
    upper, lower = packed[:count], packed[count:]
    keep_ref[...] = jnp.where(odd == 1, lower, upper)
    send_ref[...] = jnp.where(odd == 1, upper, lower)


def pack(gram):
    half = gram.shape[0] // 2
    row = lax.broadcasted_iota(jnp.int32, (half, half), 0)
    column = lax.broadcasted_iota(jnp.int32, (half, half), 1)
    last = gram[half:, half:]
    diagonal = jnp.sum(jnp.where(row == column, last, 0.0), axis=0, keepdims=True)
    extra = jnp.broadcast_to(diagonal, (SUBLANES, half))
    extra = jnp.concatenate([extra, extra], axis=1)
    body = jnp.concatenate([gram[:half, half:], jnp.where(column >= row, gram[:half, :half], last)], axis=1)
    return jnp.concatenate([body[: half // 2], extra, body[half // 2 :], extra], axis=0)


def unpack(upper, lower, work_ref):
    size = work_ref.shape[0]
    half = size // 2
    body = jnp.concatenate([upper[: half // 2], lower[: half // 2]], axis=0)
    corner, mixed = body[:, :half], body[:, half:]
    row = lax.broadcasted_iota(jnp.int32, (half, half), 0)
    column = lax.broadcasted_iota(jnp.int32, (half, half), 1)
    turned = mixed.T
    diagonal = jnp.broadcast_to(upper[half // 2 : half // 2 + 1, :half], (half, half))
    work_ref[:half, :half] = jnp.where(column >= row, mixed, turned)
    work_ref[:half, half:] = corner
    work_ref[half:, :half] = corner.T
    work_ref[half:, half:] = jnp.where(
        row == column, diagonal, jnp.where(column > row, turned, mixed)
    )


def spread(value):
    return jnp.broadcast_to(value, (SUBLANES, LANES))


def eliminate(work_ref, factor_ref, inverse_ref, panel=32, ahead=12, step=4):
    size = work_ref.shape[0]
    groups = panel // SUBLANES
    sublane = lax.broadcasted_iota(jnp.int32, (SUBLANES, LANES), 0)
    lane = lax.broadcasted_iota(jnp.int32, (SUBLANES, LANES), 1)
    wide_lane = lax.broadcasted_iota(jnp.int32, (panel, size), 1)
    chunks = range(0, size, LANES)
    for start in range(0, size, panel):
        stop = start + panel
        chunk = start // LANES * LANES
        at_chunk = chunk // LANES
        offset = start - chunk
        block = work_ref[start:stop, :]
        natural = [
            [block[i : i + SUBLANES, c : c + LANES] for c in chunks] for i in range(0, panel, SUBLANES)
        ]
        lower = [jnp.zeros((SUBLANES, LANES), F32) for _ in range(groups)]
        scale_row = jnp.zeros((SUBLANES, LANES), F32)
        scale_column = [jnp.zeros((SUBLANES, LANES), F32) for _ in range(groups)]
        columns = {}

        def keep(count):
            begin, end = len(columns), len(columns) + count
            for k in range(begin, end):
                columns[k] = {
                    g: spread(natural[g][at_chunk][:, offset + k : offset + k + 1])
                    for g in range(k // SUBLANES, groups)
                }
            kept = (lane >= offset + begin) & (lane < offset + end)
            for g in range(groups):
                identity = jnp.where(lane - offset == sublane + g * SUBLANES, 1.0, 0.0).astype(F32)
                natural[g][at_chunk] = jnp.where(kept, identity, natural[g][at_chunk])

        keep(ahead)
        pivot = spread(columns[0][0][:1, :])
        for k in range(panel):
            at, inside = divmod(k, SUBLANES)
            inverse = 1.0 / pivot
            scale = lax.rsqrt(pivot)
            ratio = {g: columns[k][g] * inverse for g in range(at, groups)}
            if k + 1 < panel:
                group, place = divmod(k + 1, SUBLANES)
                element = spread(columns[k][group][place : place + 1, :])
                pivot = spread(columns[k + 1][group][place : place + 1, :]) - element * element * inverse
            for m in range(k + 1, len(columns)):
                group, place = divmod(m, SUBLANES)
                factor = spread(ratio[group][place : place + 1, :])
                for g in range(group, groups):
                    columns[m][g] = columns[m][g] - columns[k][g] * factor
            below = dict(ratio)
            below[at] = jnp.where(sublane > inside, ratio[at], 0.0)
            for c in range(len(natural[0])):
                raw = spread(natural[at][c][inside : inside + 1, :])
                for g in range(at, groups):
                    natural[g][c] = natural[g][c] - below[g] * raw
            for g in range(at, groups):
                lower[g] = jnp.where(lane == offset + k, columns[k][g], lower[g])
            scale_row = jnp.where(lane == offset + k, scale, scale_row)
            scale_column[at] = jnp.where(sublane == inside, scale, scale_column[at])
            if (k + 1) % step == 0 and len(columns) < panel:
                keep(step)
        done = jnp.concatenate(
            [jnp.concatenate([v * scale_column[g] for v in natural[g]], axis=1) for g in range(groups)], axis=0
        )
        if stop < size:
            a, b, c = split3(done)
            left = jnp.concatenate([a, a, b, a, c, b], axis=0)
            right = jnp.concatenate([a, b, a, c, a, b], axis=0)
            first = stop // LANES * LANES
            update = rows_dot(left[:, first:], right)
            rest = work_ref[stop:, :]
            rest_lane = lax.broadcasted_iota(jnp.int32, rest.shape, 1)
            rest = jnp.where((rest_lane >= start) & (rest_lane < stop), 0.0, rest)
            work_ref[stop:, :] = rest - update[stop - first :, :]
        corner = jnp.concatenate([v * scale_row for v in lower], axis=0)
        row = lax.broadcasted_iota(jnp.int32, corner.shape, 0)
        short_lane = lax.broadcasted_iota(jnp.int32, corner.shape, 1)
        corner = jnp.where(short_lane <= row + offset, corner, 0.0)
        parts = [jnp.zeros((offset, LANES), F32), corner, jnp.zeros((LANES - offset - panel, LANES), F32)]
        turned = jnp.concatenate([v for v in parts if v.shape[0]], axis=0).T[offset : offset + panel]
        empty = jnp.zeros((panel, LANES), F32)
        turned = jnp.concatenate([turned if c == chunk else empty for c in chunks], axis=1)
        factor_ref[start:stop, :] = jnp.where(wide_lane >= stop, done, turned)
        inverse_ref[start:stop, :] = jnp.where(wide_lane < stop, done, 0.0)


def basis_kernel(
    cols_hbm_ref, mine_ref, other_ref, far_high_ref, far_low_ref, near_high_ref, near_low_ref,
    basis_ref, factor_ref, work_ref, inverse_ref, tiles_ref, held_ref, cols_ref, sems,
    *, reach, tile,
):
    odd = odd_device()
    cols_copy = pltpu.make_async_copy(cols_hbm_ref, cols_ref, sems.at[2 * reach + 1])
    cols_copy.start()
    mine, other = mine_ref[...], other_ref[...]
    unpack(jnp.where(odd == 1, other, mine), jnp.where(odd == 1, mine, other), work_ref)
    eliminate(work_ref, held_ref, inverse_ref)
    factor_copy = pltpu.make_async_copy(held_ref, factor_ref, sems.at[2 * reach])
    factor_copy.start()
    cols_copy.wait()
    high, low = split2(inverse_ref[...])
    right = jnp.concatenate([high, high, low], axis=1)
    copies = []
    for line in range(2 * reach):
        high_ref, low_ref = (far_high_ref, far_low_ref) if line < reach else (near_high_ref, near_low_ref)
        rows = slice(line % reach * tile, (line % reach + 1) * tile)
        left = jnp.concatenate([high_ref[rows, :], low_ref[rows, :], high_ref[rows, :]], axis=1)
        tiles_ref[line] = lax.dot_general(
            left, right, (((1,), (1,)), ((), ())), preferred_element_type=F32
        )
        place = pl.multiple_of(own_tile(cols_ref, odd, line, reach) * tile, tile)
        copies.append(
            pltpu.make_async_copy(tiles_ref.at[line], basis_ref.at[pl.ds(place, tile), :], sems.at[line])
        )
        copies[-1].start()
    for copy in copies:
        copy.wait()
    factor_copy.wait()


def call(kernel, outs, scratch, spaces, operands, out_spaces=None):
    operands = [
        pltpu.with_memory_space_constraint(operand, space) if space is pltpu.HBM else operand
        for operand, space in zip(operands, spaces)
    ]
    return pl.pallas_call(
        kernel,
        out_shape=outs,
        in_specs=[pl.BlockSpec(memory_space=space) for space in spaces],
        out_specs=[pl.BlockSpec(memory_space=space) for space in out_spaces or [pltpu.VMEM] * len(outs)],
        scratch_shapes=scratch,
        cost_estimate=SMALL_COST,
        compiler_params=pltpu.CompilerParams(vmem_limit_bytes=VMEM_LIMIT),
    )(*operands)


def per_device(device_count, sketch, marginal_std, cov_tiles, tile_cols):
    row_count, width = sketch.shape
    lags, tile, _ = cov_tiles.shape
    reach = (lags - 1) // 2
    halo = reach * tile
    assert row_count == 2 * halo and width % (2 * LANES) == 0
    assert device_count & (device_count - 1) == 0 and device_count > 1
    def swap(value, mask):
        return lax.ppermute(value, AXES, [(i, i ^ mask) for i in range(device_count)])

    outer_pairs = []
    for i in range(1, device_count - 1, 2):
        outer_pairs += [(i, i + 1), (i + 1, i)]
    std_rows = marginal_std.reshape(-1, LANES)

    def shape(rows, columns, dtype):
        return jax.ShapeDtypeStruct((rows, columns), dtype)

    def scaled(inner, *after):
        return call(
            functools.partial(scale_kernel, reach=reach, tile=tile, inner=inner),
            [shape(halo, width, BF16)],
            [
                pltpu.SMEM(tile_cols.shape, jnp.int32),
                pltpu.VMEM(std_rows.shape, F32),
                pltpu.VMEM((halo, width), BF16),
                pltpu.SemaphoreType.DMA((reach + 2,)),
            ],
            [pltpu.HBM] * 3 + [pl.ANY] * len(after),
            (tile_cols, std_rows, sketch, *after),
        )[0]

    outer = scaled(False)
    inner = scaled(True, outer)
    outer_halo = lax.ppermute(outer, AXES, outer_pairs)
    part = halo // HALO_PARTS
    inner_halo = [swap(inner[i : i + part], 1) for i in range(0, halo, part)]
    acc, scale, lag_block, near_high, near_low, near_gram = call(
        functools.partial(near_kernel, reach=reach, lags=lags, tile=tile),
        [
            shape(halo, width, F32),
            shape(halo, LANES, F32),
            shape(tile, halo, BF16),
            shape(halo, width, BF16),
            shape(halo, width, BF16),
            shape(width, 2 * width, F32),
        ],
        [pltpu.VMEM((tile, lags * tile), BF16), pltpu.VMEM((3 * halo, width), BF16)],
        [pltpu.SMEM] + [pltpu.VMEM] * (4 + HALO_PARTS),
        (tile_cols, cov_tiles, std_rows, outer, inner, *inner_halo),
    )
    far_high, far_low, keep, send = call(
        functools.partial(far_kernel, reach=reach, tile=tile, total=row_count * device_count),
        [
            shape(halo, width, BF16),
            shape(halo, width, BF16),
            shape(width // 4 + SUBLANES, width, F32),
            shape(width // 4 + SUBLANES, width, F32),
        ],
        [],
        [pltpu.VMEM] * 5,
        (lag_block, scale, acc, outer_halo, near_gram),
    )
    gram = keep + swap(send, 1)
    bits = [1 << i for i in range(1, device_count.bit_length() - 1)]
    if len(bits) % 2:
        gram = gram + swap(gram, bits.pop())
    rounds = [(bits[i], bits[i + 1]) for i in range(0, len(bits), 2)]
    middle = len(rounds) // 2

    def partners(pair):
        masks = (pair[0], pair[1], pair[0] | pair[1])
        return masks if pair is rounds[-1] else masks[::-1]

    for even, odd_one in zip(rounds[middle:] + rounds[:middle], rounds):
        first, second, third = (
            lax.ppermute(
                gram, AXES, [(i, i ^ (odd_mask if i % 2 else even_mask)) for i in range(device_count)]
            )
            for even_mask, odd_mask in zip(partners(even), partners(odd_one))
        )
        gram = (gram + second) + (first + third)
    other = swap(gram, 1)
    basis, factor = call(
        functools.partial(basis_kernel, reach=reach, tile=tile),
        [shape(row_count, width, F32), shape(width, width, F32)],
        [
            pltpu.VMEM((width, width), F32),
            pltpu.VMEM((width, width), F32),
            pltpu.VMEM((2 * reach, tile, width), F32),
            pltpu.VMEM((width, width), F32),
            pltpu.SMEM(tile_cols.shape, jnp.int32),
            pltpu.SemaphoreType.DMA((2 * reach + 2,)),
        ],
        [pltpu.HBM] + [pltpu.VMEM] * 6,
        (tile_cols, gram, other, far_high, far_low, near_high, near_low),
        [pl.ANY] * 2,
    )
    return basis, factor


def solution(mesh):
    device_count = mesh.shape["grp"] * mesh.shape["dev"]
    in_specs = (P(AXES, None), P(AXES), P(), P(AXES, None))
    out_specs = (P(AXES, None), P())
    return jax.shard_map(
        functools.partial(per_device, device_count),
        mesh=mesh,
        in_specs=in_specs,
        out_specs=out_specs,
        check_vma=False,
    )
```

```python
import functools

import jax
import jax.numpy as jnp
from jax import lax
from jax.experimental import pallas as pl
from jax.experimental.pallas import tpu as pltpu
from jax.sharding import PartitionSpec as P

AXES = ("grp", "dev")
F32 = jnp.float32
BF16 = jnp.bfloat16
LANES = 128
SUBLANES = 8
VMEM_LIMIT = 48 * 1024 * 1024
HALO_PARTS = 2
SMALL_COST = pl.CostEstimate(flops=1, bytes_accessed=1, transcendentals=0)


def rows_dot(left, right):
    return lax.dot_general(left, right, (((0,), (0,)), ((), ())), preferred_element_type=F32)


def split2(value):
    high = value.astype(BF16)
    return high, (value - high.astype(F32)).astype(BF16)


def split3(value):
    high = value.astype(BF16)
    rest = value - high.astype(F32)
    middle = rest.astype(BF16)
    return high, middle, (rest - middle.astype(F32)).astype(BF16)


def std_column(std_ref, index, tile, width):
    rows = tile // LANES
    parts = [
        jnp.broadcast_to(std_ref[pl.ds(index * rows + i, 1), :], (LANES, LANES)).T for i in range(rows)
    ]
    column = jnp.concatenate(parts, axis=0)
    return jnp.concatenate([column] * (width // LANES), axis=1)


def own_tile(cols_ref, odd, line, reach):
    count = 2 * reach
    line = jnp.where(odd == 1, count - 1 - line, line)
    half = line // reach
    first = half * reach
    start = cols_ref[first, reach]
    place = jnp.int32(0)
    for e in range(reach):
        place = place + jnp.where(cols_ref[first, e] >= start, 1, 0)
    return cols_ref[first, reach - place + line % reach] - cols_ref[0, reach]


def odd_device():
    return lax.rem(lax.axis_index(AXES), 2)


def scale_kernel(cols_hbm_ref, std_hbm_ref, sketch_ref, *refs, reach, tile, inner):
    out_ref, cols_ref, std_ref, rows_ref, sems = refs[-5:]
    odd = odd_device()
    first = jnp.where(odd == (0 if inner else 1), reach, 0)
    cols_copy = pltpu.make_async_copy(cols_hbm_ref, cols_ref, sems.at[reach])
    std_copy = pltpu.make_async_copy(std_hbm_ref, std_ref, sems.at[reach + 1])
    copies = []
    for i in range(reach):
        place = pl.multiple_of((first + i) * tile, tile)
        target = rows_ref.at[pl.ds(i * tile, tile), :]
        copies.append(pltpu.make_async_copy(sketch_ref.at[pl.ds(place, tile), :], target, sems.at[i]))
    for copy in (std_copy, cols_copy, *copies):
        copy.start()
    std_copy.wait()
    columns = [std_column(std_ref, first + i, tile, out_ref.shape[1]) for i in range(reach)]
    cols_copy.wait()
    for i in range(reach):
        line = jnp.int32(0)
        for e in range(reach):
            line = line + jnp.where(cols_ref[first + i, e] >= cols_ref[first, reach], 1, 0)
        line = jnp.where(odd == 1, reach - 1 - line, line)
        copies[i].wait()
        place = pl.multiple_of(line * tile, tile)
        rows = rows_ref[i * tile : (i + 1) * tile, :].astype(F32)
        out_ref[pl.ds(place, tile), :] = (rows * columns[i]).astype(BF16)


def near_kernel(
    cols_ref, cov_ref, std_ref, outer_ref, inner_ref, *refs, reach, lags, tile
):
    halo_refs = refs[:HALO_PARTS]
    acc_ref, scale_ref, lag_ref, high_ref, low_ref, gram_ref, lags_ref, lines_ref = refs[HALO_PARTS:]
    odd = odd_device()
    count = 2 * reach
    for e in range(lags):
        lags_ref[:, e * tile : (e + 1) * tile] = cov_ref[jnp.where(odd == 1, lags - 1 - e, e)]
    for e in range(reach):
        lag_ref[:, e * tile : (e + 1) * tile] = lags_ref[:, (reach - 1 - e) * tile : (reach - e) * tile]
    half = reach * tile
    lines_ref[:half, :] = outer_ref[...]
    lines_ref[half : 2 * half, :] = inner_ref[...]
    part = half // HALO_PARTS
    for line in range(reach):
        place = (reach - 1 - line) * tile
        source = halo_refs[place // part]
        lines_ref[2 * half + line * tile : 2 * half + (line + 1) * tile, :] = source[
            place % part : place % part + tile, :
        ]
    for line in range(count):
        first = max(0, reach - line)
        start = max(0, line - reach) * tile
        product = jnp.dot(
            lags_ref[:, first * tile :],
            lines_ref[start : start + (lags - first) * tile, :],
            preferred_element_type=F32,
        )
        own = own_tile(cols_ref, odd, line, reach)
        if line < reach:
            rows = slice(line * tile, (line + 1) * tile)
            acc_ref[rows, :] = product
            scale_ref[rows, :] = std_column(std_ref, own, tile, LANES)
        else:
            rows = slice((line - reach) * tile, (line - reach + 1) * tile)
            high, low = split2(product * std_column(std_ref, own, tile, product.shape[1]))
            high_ref[rows, :] = high
            low_ref[rows, :] = low
    gram_ref[...] = rows_dot(
        high_ref[...], jnp.concatenate([high_ref[...], low_ref[...]], axis=1)
    )


def far_kernel(
    lag_ref, scale_ref, acc_ref, halo_ref, gram_ref, high_ref, low_ref, keep_ref, send_ref,
    *, reach, tile, total,
):
    odd = odd_device()
    width = acc_ref.shape[1]
    for line in range(reach):
        rows = slice(line * tile, (line + 1) * tile)
        product = acc_ref[rows, :] + jnp.dot(
            lag_ref[:, line * tile :],
            halo_ref[: (reach - line) * tile, :],
            preferred_element_type=F32,
        )
        scale = jnp.concatenate([scale_ref[rows, :]] * (width // LANES), axis=1)
        high, low = split2(product * scale)
        high_ref[rows, :] = high
        low_ref[rows, :] = low
    both = gram_ref[...] + rows_dot(
        high_ref[...], jnp.concatenate([high_ref[...], low_ref[...]], axis=1)
    )
    cross = both[:, width:]
    gram = (both[:, :width] + (cross + cross.T)) * (1.0 / total)
    packed = pack(gram)
    count = packed.shape[0] // 2
    upper, lower = packed[:count], packed[count:]
    keep_ref[...] = jnp.where(odd == 1, lower, upper)
    send_ref[...] = jnp.where(odd == 1, upper, lower)


def pack(gram):
    half = gram.shape[0] // 2
    row = lax.broadcasted_iota(jnp.int32, (half, half), 0)
    column = lax.broadcasted_iota(jnp.int32, (half, half), 1)
    last = gram[half:, half:]
    diagonal = jnp.sum(jnp.where(row == column, last, 0.0), axis=0, keepdims=True)
    extra = jnp.broadcast_to(diagonal, (SUBLANES, half))
    extra = jnp.concatenate([extra, extra], axis=1)
    body = jnp.concatenate([gram[:half, half:], jnp.where(column >= row, gram[:half, :half], last)], axis=1)
    return jnp.concatenate([body[: half // 2], extra, body[half // 2 :], extra], axis=0)


def unpack(upper, lower, work_ref):
    size = work_ref.shape[0]
    half = size // 2
    body = jnp.concatenate([upper[: half // 2], lower[: half // 2]], axis=0)
    corner, mixed = body[:, :half], body[:, half:]
    row = lax.broadcasted_iota(jnp.int32, (half, half), 0)
    column = lax.broadcasted_iota(jnp.int32, (half, half), 1)
    turned = mixed.T
    diagonal = jnp.broadcast_to(upper[half // 2 : half // 2 + 1, :half], (half, half))
    work_ref[:half, :half] = jnp.where(column >= row, mixed, turned)
    work_ref[:half, half:] = corner
    work_ref[half:, :half] = jnp.zeros((half, half), F32)
    work_ref[half:, half:] = jnp.where(
        row == column, diagonal, jnp.where(column > row, turned, mixed)
    )


def spread(value):
    return jnp.broadcast_to(value, (SUBLANES, LANES))


def eliminate(work_ref, factor_ref, inverse_ref, panel=32, ahead=12, step=4):
    size = work_ref.shape[0]
    groups = panel // SUBLANES
    sublane = lax.broadcasted_iota(jnp.int32, (SUBLANES, LANES), 0)
    lane = lax.broadcasted_iota(jnp.int32, (SUBLANES, LANES), 1)
    wide_lane = lax.broadcasted_iota(jnp.int32, (panel, size), 1)
    chunks = range(0, size, LANES)
    for start in range(0, size, panel):
        stop = start + panel
        chunk = start // LANES * LANES
        at_chunk = chunk // LANES
        offset = start - chunk
        block = work_ref[start:stop, :]
        natural = [
            [block[i : i + SUBLANES, c : c + LANES] for c in chunks] for i in range(0, panel, SUBLANES)
        ]
        lower = [jnp.zeros((SUBLANES, LANES), F32) for _ in range(groups)]
        scale_row = jnp.zeros((SUBLANES, LANES), F32)
        scale_column = [jnp.zeros((SUBLANES, LANES), F32) for _ in range(groups)]
        columns = {}

        def keep(count):
            begin, end = len(columns), len(columns) + count
            for k in range(begin, end):
                columns[k] = {
                    g: spread(natural[g][at_chunk][:, offset + k : offset + k + 1])
                    for g in range(k // SUBLANES, groups)
                }
            kept = (lane >= offset + begin) & (lane < offset + end)
            for g in range(groups):
                identity = jnp.where(lane - offset == sublane + g * SUBLANES, 1.0, 0.0).astype(F32)
                natural[g][at_chunk] = jnp.where(kept, identity, natural[g][at_chunk])

        keep(ahead)
        pivot = spread(columns[0][0][:1, :])
        for k in range(panel):
            at, inside = divmod(k, SUBLANES)
            inverse = 1.0 / pivot
            scale = lax.rsqrt(pivot)
            ratio = {g: columns[k][g] * inverse for g in range(at, groups)}
            if k + 1 < panel:
                group, place = divmod(k + 1, SUBLANES)
                element = spread(columns[k][group][place : place + 1, :])
                pivot = spread(columns[k + 1][group][place : place + 1, :]) - element * element * inverse
            for m in range(k + 1, len(columns)):
                group, place = divmod(m, SUBLANES)
                factor = spread(ratio[group][place : place + 1, :])
                for g in range(group, groups):
                    columns[m][g] = columns[m][g] - columns[k][g] * factor
            below = dict(ratio)
            below[at] = jnp.where(sublane > inside, ratio[at], 0.0)
            for c in range(len(natural[0])):
                raw = spread(natural[at][c][inside : inside + 1, :])
                for g in range(at, groups):
                    natural[g][c] = natural[g][c] - below[g] * raw
            for g in range(at, groups):
                lower[g] = jnp.where(lane == offset + k, columns[k][g], lower[g])
            scale_row = jnp.where(lane == offset + k, scale, scale_row)
            scale_column[at] = jnp.where(sublane == inside, scale, scale_column[at])
            if (k + 1) % step == 0 and len(columns) < panel:
                keep(step)
        done = jnp.concatenate(
            [jnp.concatenate([v * scale_column[g] for v in natural[g]], axis=1) for g in range(groups)], axis=0
        )
        if stop < size:
            a, b, c = split3(done)
            left = jnp.concatenate([a, a, b, a, c, b], axis=0)
            right = jnp.concatenate([a, b, a, c, a, b], axis=0)
            first = stop // LANES * LANES
            update = rows_dot(left[:, first:], right)
            rest = work_ref[stop:, :]
            rest_lane = lax.broadcasted_iota(jnp.int32, rest.shape, 1)
            rest = jnp.where((rest_lane >= start) & (rest_lane < stop), 0.0, rest)
            work_ref[stop:, :] = rest - update[stop - first :, :]
        corner = jnp.concatenate([v * scale_row for v in lower], axis=0)
        row = lax.broadcasted_iota(jnp.int32, corner.shape, 0)
        short_lane = lax.broadcasted_iota(jnp.int32, corner.shape, 1)
        corner = jnp.where(short_lane <= row + offset, corner, 0.0)
        parts = [jnp.zeros((offset, LANES), F32), corner, jnp.zeros((LANES - offset - panel, LANES), F32)]
        turned = jnp.concatenate([v for v in parts if v.shape[0]], axis=0).T[offset : offset + panel]
        empty = jnp.zeros((panel, LANES), F32)
        turned = jnp.concatenate([turned if c == chunk else empty for c in chunks], axis=1)
        factor_ref[start:stop, :] = jnp.where(wide_lane >= stop, done, turned)
        high, low = split2(jnp.where(wide_lane < stop, done, 0.0))
        inverse_ref[start:stop, :] = jnp.concatenate([high, high, low], axis=1)


def basis_kernel(
    cols_hbm_ref, mine_ref, other_ref, far_high_ref, far_low_ref, near_high_ref, near_low_ref,
    basis_ref, factor_ref, work_ref, inverse_ref, tiles_ref, held_ref, cols_ref, sems,
    *, reach, tile,
):
    odd = odd_device()
    cols_copy = pltpu.make_async_copy(cols_hbm_ref, cols_ref, sems.at[2 * reach])
    cols_copy.start()
    mine, other = mine_ref[...], other_ref[...]
    unpack(jnp.where(odd == 1, other, mine), jnp.where(odd == 1, mine, other), work_ref)
    eliminate(work_ref, held_ref, inverse_ref)
    copies = [pltpu.make_async_copy(held_ref, factor_ref, sems.at[2 * reach + 1])]
    cols_copy.wait()
    right = inverse_ref[...]
    for line in range(2 * reach):
        high_ref, low_ref = (far_high_ref, far_low_ref) if line < reach else (near_high_ref, near_low_ref)
        rows = slice(line % reach * tile, (line % reach + 1) * tile)
        left = jnp.concatenate([high_ref[rows, :], low_ref[rows, :], high_ref[rows, :]], axis=1)
        tiles_ref[line] = lax.dot_general(
            left, right, (((1,), (1,)), ((), ())), preferred_element_type=F32
        )
        place = pl.multiple_of(own_tile(cols_ref, odd, line, reach) * tile, tile)
        copies.append(
            pltpu.make_async_copy(tiles_ref.at[line], basis_ref.at[pl.ds(place, tile), :], sems.at[line])
        )
        copies[-1].start()
        if line == 0:
            copies[0].start()
    for copy in copies:
        copy.wait()


def call(kernel, outs, scratch, spaces, operands, out_spaces=None):
    operands = [
        pltpu.with_memory_space_constraint(operand, space) if space is pltpu.HBM else operand
        for operand, space in zip(operands, spaces)
    ]
    return pl.pallas_call(
        kernel,
        out_shape=outs,
        in_specs=[pl.BlockSpec(memory_space=space) for space in spaces],
        out_specs=[pl.BlockSpec(memory_space=space) for space in out_spaces or [pltpu.VMEM] * len(outs)],
        scratch_shapes=scratch,
        cost_estimate=SMALL_COST,
        compiler_params=pltpu.CompilerParams(vmem_limit_bytes=VMEM_LIMIT),
    )(*operands)


def per_device(device_count, sketch, marginal_std, cov_tiles, tile_cols):
    row_count, width = sketch.shape
    lags, tile, _ = cov_tiles.shape
    reach = (lags - 1) // 2
    halo = reach * tile
    assert row_count == 2 * halo and width % (2 * LANES) == 0
    assert device_count & (device_count - 1) == 0 and device_count > 1
    def swap(value, mask):
        return lax.ppermute(value, AXES, [(i, i ^ mask) for i in range(device_count)])

    outer_pairs = []
    for i in range(1, device_count - 1, 2):
        outer_pairs += [(i, i + 1), (i + 1, i)]
    std_rows = marginal_std.reshape(-1, LANES)

    def shape(rows, columns, dtype):
        return jax.ShapeDtypeStruct((rows, columns), dtype)

    def scaled(inner, *after):
        return call(
            functools.partial(scale_kernel, reach=reach, tile=tile, inner=inner),
            [shape(halo, width, BF16)],
            [
                pltpu.SMEM(tile_cols.shape, jnp.int32),
                pltpu.VMEM(std_rows.shape, F32),
                pltpu.VMEM((halo, width), BF16),
                pltpu.SemaphoreType.DMA((reach + 2,)),
            ],
            [pltpu.HBM] * 3 + [pl.ANY] * len(after),
            (tile_cols, std_rows, sketch, *after),
        )[0]

    outer = scaled(False)
    inner = scaled(True, outer)
    outer_halo = lax.ppermute(outer, AXES, outer_pairs)
    part = halo // HALO_PARTS
    inner_halo = [swap(inner[i : i + part], 1) for i in range(0, halo, part)]
    acc, scale, lag_block, near_high, near_low, near_gram = call(
        functools.partial(near_kernel, reach=reach, lags=lags, tile=tile),
        [
            shape(halo, width, F32),
            shape(halo, LANES, F32),
            shape(tile, halo, BF16),
            shape(halo, width, BF16),
            shape(halo, width, BF16),
            shape(width, 2 * width, F32),
        ],
        [pltpu.VMEM((tile, lags * tile), BF16), pltpu.VMEM((3 * halo, width), BF16)],
        [pltpu.SMEM] + [pltpu.VMEM] * (4 + HALO_PARTS),
        (tile_cols, cov_tiles, std_rows, outer, inner, *inner_halo),
    )
    far_high, far_low, keep, send = call(
        functools.partial(far_kernel, reach=reach, tile=tile, total=row_count * device_count),
        [
            shape(halo, width, BF16),
            shape(halo, width, BF16),
            shape(width // 4 + SUBLANES, width, F32),
            shape(width // 4 + SUBLANES, width, F32),
        ],
        [],
        [pltpu.VMEM] * 5,
        (lag_block, scale, acc, outer_halo, near_gram),
    )
    gram = keep + swap(send, 1)
    bits = [1 << i for i in range(1, device_count.bit_length() - 1)]
    if len(bits) % 2:
        gram = gram + swap(gram, bits.pop())
    rounds = [(bits[i], bits[i + 1]) for i in range(0, len(bits), 2)]
    middle = len(rounds) // 2

    def partners(pair):
        masks = (pair[0], pair[1], pair[0] | pair[1])
        return masks if pair is rounds[-1] else masks[::-1]

    for even, odd_one in zip(rounds[middle:] + rounds[:middle], rounds):
        first, second, third = (
            lax.ppermute(
                gram, AXES, [(i, i ^ (odd_mask if i % 2 else even_mask)) for i in range(device_count)]
            )
            for even_mask, odd_mask in zip(partners(even), partners(odd_one))
        )
        gram = (gram + second) + (first + third)
    other = swap(gram, 1)
    basis, factor = call(
        functools.partial(basis_kernel, reach=reach, tile=tile),
        [shape(row_count, width, F32), shape(width, width, F32)],
        [
            pltpu.VMEM((width, width), F32),
            pltpu.VMEM((width, 3 * width), BF16),
            pltpu.VMEM((2 * reach, tile, width), F32),
            pltpu.VMEM((width, width), F32),
            pltpu.SMEM(tile_cols.shape, jnp.int32),
            pltpu.SemaphoreType.DMA((2 * reach + 2,)),
        ],
        [pltpu.HBM] + [pltpu.VMEM] * 6,
        (tile_cols, gram, other, far_high, far_low, near_high, near_low),
        [pl.ANY] * 2,
    )
    return basis, factor


def solution(mesh):
    device_count = mesh.shape["grp"] * mesh.shape["dev"]
    in_specs = (P(AXES, None), P(AXES), P(), P(AXES, None))
    out_specs = (P(AXES, None), P())
    return jax.shard_map(
        functools.partial(per_device, device_count),
        mesh=mesh,
        in_specs=in_specs,
        out_specs=out_specs,
        check_vma=False,
    )
```
